512 devices in a mesh: dp: 32 (over z, x_hi, core), comp: 16 (over x_lo, y).
Axes of the slice: x: 4 (x_hi: 2, x_lo: 2; x = x_hi * 2 + x_lo), y: 8, z: 8, core: 2. Of those that a mesh axis runs over, the one named last changes fastest.
Arguments:
- embeddings: float32 [32768, 768], P('dp'), may hold values from -6 to 6
- comp_means: float32 [8192, 768], P(('comp', 'dp')), may hold values from -1.2 to 1.2
- comp_variances: float32 [8192, 768], P(('comp', 'dp')), may hold values from 0.8 to 1.25
- comp_mass: float32 [8192], P(('comp', 'dp')), may hold values from 0.3 to 3
Outputs:
- new_means: float32 [8192, 768], P(('comp', 'dp'))
- new_variances: float32 [8192, 768], P(('comp', 'dp'))
- new_mass: float32 [8192], P(('comp', 'dp'))
The draws below stay inside these ranges and needn't reach their ends.
All inputs are finite; a program needn't handle non-finite values.
Results may differ from the reference program's by a relative error of at most 0.0003.
Values sent between devices are 32-bit elements; how exact they have to be, the bound alone decides.
A program may use at most 64 MiB of HBM per device.

```python
import math
import jax
import jax.numpy as jnp
from jax import lax

D = 768
ROW_DEV = 1024
K = 8192
ROWS = 32768
N_DP = 32


def draw_embeddings(key, part):
    key_main = jax.random.fold_in(key, 11)
    values_drawn = jax.random.normal(key_main, (ROWS, D), jnp.float32)
    return jnp.clip(values_drawn, -6.0, 6.0)


def block_levels(key, extent, pieces, least, high):
    factor_of = 1.0
    for dim, shards_of in pieces:
        draws = jax.random.uniform(jax.random.fold_in(jax.random.fold_in(key, 6), dim), (shards_of,), jnp.float32, least / len(pieces), high / len(pieces))
        factor_of = factor_of * jnp.repeat(jnp.exp(draws), extent[dim] // shards_of).reshape((-1,) + (1,) * (len(extent) - 1 - dim))
    return factor_of


def bell_draw(own_key, shape, scale, bound, cuts=(), dtype=jnp.bfloat16):
    values = jax.random.normal(own_key, shape, jnp.float32) * scale
    if len(cuts) > 0:
        values = block_levels(own_key, shape, cuts, -0.22, 0.18) * values
    return jnp.clip(values, min=-bound, max=bound).astype(dtype)


def setup_inputs(seed: int = 0) -> dict:
    seeds = jax.random.split(jax.random.key(seed), 5)
    embeddings = draw_embeddings(jax.random.fold_in(seeds[4], 71), 0)
    comp_means = bell_draw(seeds[1], (K, D), 0.2, 1.2, ((0, 512),), jnp.float32)
    comp_variances = jnp.clip(jnp.exp(math.log(1.25) - 0.4462871 * jax.random.uniform(seeds[2], (K, D), jnp.float32) ** block_levels(seeds[2], (K, D), ((0, 512),), -0.2, 0.2)), 0.8, 1.25)
    comp_mass = jnp.clip(jnp.exp(math.log(3.0) - 2.3025851 * jax.random.uniform(seeds[3], (K,), jnp.float32) ** block_levels(seeds[3], (K,), ((0, 512),), -0.2, 0.2)), 0.3, 3.0)
    return {"embeddings": embeddings, "comp_means": comp_means, "comp_variances": comp_variances, "comp_mass": comp_mass}


def coefficients(comp_means, comp_variances, comp_mass):
    precision = 1.0 / comp_variances
    neg_half = -0.5 * precision
    mean_prec = comp_means * precision
    offset = jnp.log(comp_mass) - 0.5 * jnp.sum(jnp.log(comp_variances) + comp_means * mean_prec, axis=1)
    return neg_half, mean_prec, offset


def scores_of(row_block, squares, neg_half, mean_prec, offset):
    highest = lax.Precision.HIGHEST
    quad = jnp.dot(squares, neg_half.T, precision=highest, preferred_element_type=jnp.float32)
    linear = jnp.dot(row_block, mean_prec.T, precision=highest, preferred_element_type=jnp.float32)
    return quad + linear + offset[None, :]


def moments_of(responsibility, values):
    return lax.dot_general(responsibility, values, (((0,), (0,)), ((), ())), precision=lax.Precision.HIGHEST, preferred_element_type=jnp.float32)


def reference(embeddings, comp_means, comp_variances, comp_mass):
    neg_half, mean_prec, offset = coefficients(comp_means, comp_variances, comp_mass)
    blocks = embeddings.reshape(N_DP, ROW_DEV, D)

    def accumulate(running, row_block):
        squares = row_block * row_block
        scores = scores_of(row_block, squares, neg_half, mean_prec, offset)
        row_peak = jnp.max(scores, axis=1, keepdims=True)
        shifted = jnp.exp(scores - row_peak)
        row_total = jnp.sum(shifted, axis=1, keepdims=True)
        responsibility = shifted / row_total
        first_sums = running[0] + moments_of(responsibility, row_block)
        second_sums = running[1] + moments_of(responsibility, squares)
        counts = running[2] + jnp.sum(responsibility, axis=0)
        return (first_sums, second_sums, counts), None

    initial = (jnp.zeros((K, D), jnp.float32), jnp.zeros((K, D), jnp.float32), jnp.zeros((K,), jnp.float32))
    totals, unused = lax.scan(accumulate, initial, blocks)
    first_sums, second_sums, counts = totals
    mass_scale = K / ROWS
    new_mass = 0.4 * comp_mass + 0.6 * mass_scale * counts
    first_moment = 0.4 * comp_mass[:, None] * comp_means + 0.6 * mass_scale * first_sums
    second_moment = 0.4 * comp_mass[:, None] * (comp_variances + comp_means * comp_means) + 0.6 * mass_scale * second_sums
    new_means = first_moment / new_mass[:, None]
    new_variances = second_moment / new_mass[:, None] - new_means * new_means
    return (new_means, new_variances, new_mass)
```

```python
import functools

import jax
import jax.numpy as jnp
from jax import lax
from jax.experimental import pallas as pl
from jax.experimental.pallas import tpu as pltpu
from jax.sharding import PartitionSpec as P

MESH = pl.DeviceIdType.MESH
NT = (((1,), (1,)), ((), ()))
NN = (((1,), (0,)), ((), ()))


def split(value):
    high = value.astype(jnp.bfloat16)
    return high, (value - high.astype(jnp.float32)).astype(jnp.bfloat16)


def kernel(
    n_z, n_comp, mass_scale,
    emb_hbm, mean_ref, var_ref, mass_ref,
    new_mean_ref, new_var_ref, new_mass_ref,
    emb, wbuf, lhs, offs, xx_hi, xx_lo, st, stats, fac, rt,
    mbuf, sbuf, rbuf, lbuf, xbuf,
    emb_sem, gs, gr, ss, sr, ms, mr,
):
    f32 = jnp.float32
    rows, width = emb.shape
    own = mean_ref.shape[0]
    chunk = 2 * own
    half = n_z * chunk
    tiles = rows // 128
    dp, comp = lax.axis_index("dp"), lax.axis_index("comp")
    z, xh, core = dp // 4, (dp // 2) % 2, dp % 2
    other_x, other_core = 1 - xh, 1 - core

    def at(zz, xx, cc):
        return (zz * 4 + xx * 2 + cc, comp)

    def z_off(k):
        return (z + k + n_z) % n_z

    right, left = at(z_off(1), xh, core), at(z_off(-1), xh, core)
    partner, sibling = at(z, other_x, core), at(z, xh, other_core)

    emb_copy = pltpu.make_async_copy(emb_hbm, emb, emb_sem)
    emb_copy.start()
    barrier = pltpu.get_barrier_semaphore()
    for target in (right, left, partner, sibling):
        pl.semaphore_signal(barrier, inc=1, device_id=target, device_id_type=MESH)

    def greet(t, carry):
        peer = (dp, (comp + t) % n_comp)
        pl.semaphore_signal(barrier, inc=1, device_id=peer, device_id_type=MESH)
        return carry

    lax.fori_loop(1, n_comp, greet, 0)

    means, variances = mean_ref[...], var_ref[...]
    precision = 1.0 / variances
    mean_prec = means * precision
    diagonal = lax.broadcasted_iota(jnp.int32, (own, own), 0) == lax.broadcasted_iota(
        jnp.int32, (own, own), 1
    )
    mass = jnp.sum(
        jnp.where(diagonal, jnp.broadcast_to(mass_ref[...], (own, own)), 0.0), axis=1, keepdims=True
    )
    offset = jnp.log(mass) - 0.5 * jnp.sum(
        jnp.log(variances) + means * mean_prec, axis=1, keepdims=True
    )

    def w_rows(cc, zz, xx):
        return pl.ds(pl.multiple_of(cc * half + zz * chunk + xx * own, own), own)

    mine = w_rows(core, z, xh)
    wbuf[mine, 0:width] = -0.5 * precision
    wbuf[mine, width : 2 * width] = mean_prec
    wbuf[mine, 2 * width :] = jnp.broadcast_to(offset, (own, 128))

    pl.semaphore_wait(barrier, 4 + n_comp - 1)

    cols = (xh, other_x)

    def gather_copy(index, zz, c, target):
        place = w_rows(core, zz, cols[c])
        return pltpu.make_async_remote_copy(
            src_ref=wbuf.at[place], dst_ref=wbuf.at[place],
            send_sem=gs.at[index], recv_sem=gr.at[index],
            device_id=target, device_id_type=MESH,
        )

    def r_index(step, c):
        return 1 + (step - 1) * 2 + c

    def l_index(step, c):
        return 8 + (step - 1) * 2 + (c if step < 4 else 0)

    def s_index(k, c):
        return 15 + (k % 8) * 2 + c

    sent = []

    def send(index, zz, c, target):
        copy = gather_copy(index, zz, c, target)
        copy.start()
        sent.append(copy)

    def arrived(index):
        gather_copy(index, z, 0, partner).wait_recv()

    def to_sibling(k, c):
        send(s_index(k, c), z_off(k), c, sibling)

    send(r_index(1, 0), z, 0, right)
    send(l_index(1, 0), z, 0, left)
    send(0, z, 0, partner)
    to_sibling(0, 0)

    emb_copy.wait()

    def prepare(i, carry):
        place = pl.ds(pl.multiple_of(i * 128, 128), 128)
        x = emb[place, :]
        hi, lo = split(x * x)
        xx_hi[place, 0:width] = hi
        xx_lo[place, 0:width] = lo
        hi, lo = split(x)
        xx_hi[place, width:] = hi
        xx_lo[place, width:] = lo
        return carry

    lax.fori_loop(0, tiles, prepare, 0)

    sizes = (2 * chunk, 4 * chunk, 4 * chunk, 4 * chunk, 2 * chunk)
    bases = (0, 2 * chunk, 6 * chunk, 10 * chunk, 14 * chunk)

    def places(k):
        shifts = (k,) if k in (0, 4) else (-k, k)
        return [(cc, z_off(s)) for cc in (core, other_core) for s in shifts]

    def stage(k):
        n, base = sizes[k], bases[k]
        for i, (cc, zz) in enumerate(places(k)):
            place = pl.ds(pl.multiple_of(cc * half + zz * chunk, chunk), chunk)
            hi, lo = split(wbuf[place, 0 : 2 * width])
            lhs[i * chunk : (i + 1) * chunk, :] = hi
            lhs[n + i * chunk : n + (i + 1) * chunk, :] = lo
            offs[base + i * chunk : base + (i + 1) * chunk, :] = wbuf[place, 2 * width :]

    block = 256

    def score(k):
        n, base = sizes[k], bases[k]

        def body(b, carry):
            place = pl.ds(pl.multiple_of(b * block, block), block)
            both = lax.dot_general(
                lhs[0 : 2 * n, :], xx_hi[place, :], NT, preferred_element_type=f32
            )
            low = lax.dot_general(lhs[0:n, :], xx_lo[place, :], NT, preferred_element_type=f32)
            off = offs[base : base + n, :]
            st[base : base + n, place] = both[:n] + both[n:] + low + jnp.concatenate([off, off], 1)
            return carry

        lax.fori_loop(0, rows // block, body, 0)

    def sibling_arrived(ks):
        for k in ks:
            for c in range(2):
                arrived(s_index(k, c))

    arrived(0)
    send(r_index(1, 1), z, 1, right)
    send(l_index(1, 1), z, 1, left)
    to_sibling(0, 1)
    for step in range(1, 4):
        for c in range(2):
            arrived(r_index(step, c))
            if step < 3 or c == 0:
                send(r_index(step + 1, c), z_off(-step), c, right)
            arrived(l_index(step, c))
            if step < 3 or c == 1:
                send(l_index(step + 1, c), z_off(step), c, left)
            to_sibling(-step, c)
            to_sibling(step, c)
            if c == 0:
                if step == 1:
                    sibling_arrived((0,))
                else:
                    sibling_arrived((1 - step, step - 1))
                stage(step - 1)
                score(step - 1)
    sibling_arrived((-3, 3))
    stage(3)
    score(3)
    arrived(r_index(4, 0))
    to_sibling(4, 0)
    arrived(l_index(4, 1))
    to_sibling(4, 1)
    sibling_arrived((4,))
    stage(4)
    score(4)

    for i in range(tiles):
        lanes = slice(i * 128, (i + 1) * 128)
        s = st[:, lanes]
        peak = jnp.max(s, axis=0, keepdims=True)
        e = jnp.exp(s - peak)
        st[:, lanes] = e
        stats[comp, i : i + 1, :] = peak
        stats[comp, tiles + i : tiles + i + 1, :] = jnp.sum(e, axis=0, keepdims=True)

    def stat_copy(t):
        return pltpu.make_async_remote_copy(
            src_ref=stats.at[comp], dst_ref=stats.at[comp],
            send_sem=ss.at[t], recv_sem=sr.at[t],
            device_id=(dp, (comp + t) % n_comp), device_id_type=MESH,
        )

    def stat_start(t, carry):
        stat_copy(t).start()
        return carry

    def stat_wait(t, carry):
        stat_copy(t).wait_recv()
        return carry

    lax.fori_loop(1, n_comp, stat_start, 0)
    lax.fori_loop(1, n_comp, stat_wait, 0)
    peaks, totals = stats[:, 0:tiles, :], stats[:, tiles:, :]
    peak = jnp.max(peaks, axis=0)
    total = jnp.sum(totals * jnp.exp(peaks - peak[None]), axis=0)
    fac[...] = jnp.exp(stats[comp, 0:tiles, :] - peak) / total

    counts = None
    for i in range(tiles):
        lanes = slice(i * 128, (i + 1) * 128)
        resp = st[:, lanes] * fac[i : i + 1, :]
        counts = resp if counts is None else counts + resp
        hi, lo = split(resp)
        for n, base in zip(sizes, bases):
            rt[2 * base : 2 * base + n, lanes] = hi[base : base + n]
            rt[2 * base + n : 2 * base + 2 * n, lanes] = lo[base : base + n]
    mbuf[:, 2 * width :] = counts

    def moments(k):
        n, base = sizes[k], bases[k]

        def body(b, carry):
            lanes = pl.ds(pl.multiple_of(b * block, block), block)
            both = lax.dot_general(
                rt[2 * base : 2 * base + 2 * n, :], xx_hi[:, lanes], NN, preferred_element_type=f32
            )
            low = lax.dot_general(
                rt[2 * base : 2 * base + n, :], xx_lo[:, lanes], NN, preferred_element_type=f32
            )
            mbuf[base : base + n, lanes] = both[:n] + both[n:] + low
            return carry

        lax.fori_loop(0, 2 * width // block, body, 0)

    def reduce_copy(index, src, dst, target):
        return pltpu.make_async_remote_copy(
            src_ref=src, dst_ref=dst, send_sem=ms.at[index], recv_sem=mr.at[index],
            device_id=target, device_id_type=MESH,
        )

    def push(index, src, dst, target):
        copy = reduce_copy(index, src, dst, target)
        copy.start()
        sent.append(copy)

    def with_sibling(k):
        n, base = sizes[k], bases[k]
        h = n // 2
        theirs = mbuf.at[base + h : base + n]
        push(k, theirs, sbuf.at[base // 2 : base // 2 + h], sibling)

    def add_sibling(k):
        n, base = sizes[k], bases[k]
        h = n // 2
        landed = sbuf.at[base // 2 : base // 2 + h]
        reduce_copy(k, landed, landed, sibling).wait_recv()
        mbuf[base : base + h, :] += landed[...]

    def m_rows(k, c):
        side = 1 if 0 < k < 4 else 0
        start = bases[abs(k)] + side * chunk + cols[c] * own
        return pl.ds(pl.multiple_of(start, own), own)

    def slot(step, c):
        return 2 * (step - 1) - (1 if step > 1 else 0) + (c if step > 1 else 0)

    def pass_on(step, c, toward, buf, first, target):
        k = toward * (5 - step) if step > 1 else 4
        index = slot(step, c)
        if step == 1 or (step == 2 and c != first):
            src = mbuf.at[m_rows(k, c)]
        else:
            before = buf.at[slot(step - 1, c)]
            reduce_copy(base_of[toward] + slot(step - 1, c), before, before, target).wait_recv()
            before[...] += mbuf[m_rows(k, c), :]
            src = before
        push(base_of[toward] + index, src, buf.at[index], target)

    base_of = {1: 5, -1: 12}
    moments(4)
    with_sibling(4)
    add_sibling(4)
    pass_on(1, 0, 1, rbuf, 0, right)
    pass_on(1, 1, -1, lbuf, 1, left)
    for step in range(2, 5):
        k = 5 - step
        moments(k)
        with_sibling(k)
        add_sibling(k)
        order = (0, 1) if step > 2 else (1, 0)
        for c in order:
            pass_on(step, c, 1, rbuf, 0, right)
            pass_on(step, 1 - c if step == 2 else c, -1, lbuf, 1, left)
    moments(0)
    with_sibling(0)
    add_sibling(0)

    def collected(c):
        value = mbuf[m_rows(0, c), :]
        for toward, buf in ((1, rbuf), (-1, lbuf)):
            landed = buf.at[slot(4, c)]
            reduce_copy(base_of[toward] + slot(4, c), landed, landed, right).wait_recv()
            value += landed[...]
        return value

    mbuf[m_rows(0, 1), :] = collected(1)
    push(19, mbuf.at[m_rows(0, 1)], xbuf, partner)
    sums = collected(0)
    reduce_copy(19, xbuf, xbuf, partner).wait_recv()
    sums += xbuf[...]

    counts = jnp.sum(sums[:, 2 * width :], axis=1, keepdims=True)
    kept = 0.4 * mass
    new_mass = kept + 0.6 * mass_scale * counts
    means, variances = mean_ref[...], var_ref[...]
    first = kept * means + 0.6 * mass_scale * sums[:, width : 2 * width]
    second = kept * (variances + means * means) + 0.6 * mass_scale * sums[:, 0:width]
    new_means = first / new_mass
    new_mean_ref[...] = new_means
    new_var_ref[...] = second / new_mass - new_means * new_means
    new_mass_ref[...] = jnp.sum(
        jnp.where(diagonal, jnp.broadcast_to(new_mass, (own, own)), 0.0), axis=0, keepdims=True
    )

    for copy in sent:
        copy.wait_send()

    def stat_sent(t, carry):
        stat_copy(t).wait_send()
        return carry

    lax.fori_loop(1, n_comp, stat_sent, 0)


def solution(mesh):
    n_dp, n_comp = mesh.shape["dp"], mesh.shape["comp"]
    n_z = n_dp // 4

    def per_device(embeddings, comp_means, comp_variances, comp_mass):
        rows, width = embeddings.shape
        own = comp_means.shape[0]
        group = own * n_dp
        wide = 2 * width + 128
        tiles = rows // 128
        f32, bf16 = jnp.float32, jnp.bfloat16
        vmem, dma = pltpu.VMEM, pltpu.SemaphoreType.DMA
        inside = pl.BlockSpec(memory_space=pltpu.VMEM)
        new_means, new_variances, new_mass = pl.pallas_call(
            functools.partial(kernel, n_z, n_comp, (group * n_comp) / (rows * n_dp)),
            out_shape=[
                jax.ShapeDtypeStruct((own, width), f32),
                jax.ShapeDtypeStruct((own, width), f32),
                jax.ShapeDtypeStruct((1, own), f32),
            ],
            in_specs=[pl.BlockSpec(memory_space=pl.ANY), inside, inside, inside],
            out_specs=[inside, inside, inside],
            scratch_shapes=[
                vmem((rows, width), f32),
                vmem((group, wide), f32),
                vmem((16 * own, 2 * width), bf16),
                vmem((group, 128), f32),
                vmem((rows, 2 * width), bf16),
                vmem((rows, 2 * width), bf16),
                vmem((group, rows), f32),
                vmem((n_comp, 2 * tiles, 128), f32),
                vmem((tiles, 128), f32),
                vmem((2 * group, rows), bf16),
                vmem((group, wide), f32),
                vmem((group // 2, wide), f32),
                vmem((7, own, wide), f32),
                vmem((7, own, wide), f32),
                vmem((own, wide), f32),
                dma, dma((31,)), dma((31,)), dma((n_comp,)), dma((n_comp,)), dma((20,)), dma((20,)),
            ],
            compiler_params=pltpu.CompilerParams(
                collective_id=0, has_side_effects=True, vmem_limit_bytes=56 * 1024 * 1024
            ),
        )(embeddings, comp_means, comp_variances, comp_mass.reshape(1, own))
        return new_means, new_variances, new_mass.reshape(own)

    placed = (P("dp", None), P(("comp", "dp"), None), P(("comp", "dp"), None), P(("comp", "dp")))
    return jax.shard_map(
        per_device,
        mesh=mesh,
        in_specs=placed,
        out_specs=(P(("comp", "dp"), None), P(("comp", "dp"), None), P(("comp", "dp"))),
        check_vma=False,
    )
```

```python
import functools

import jax
import jax.numpy as jnp
from jax import lax
from jax.experimental import pallas as pl
from jax.experimental.pallas import tpu as pltpu
from jax.sharding import PartitionSpec as P

MESH = pl.DeviceIdType.MESH
NT = (((1,), (1,)), ((), ()))
NN = (((1,), (0,)), ((), ()))


def split(value):
    high = value.astype(jnp.bfloat16)
    return high, (value - high.astype(jnp.float32)).astype(jnp.bfloat16)


def diagonal(n):
    return lax.broadcasted_iota(jnp.int32, (n, n), 0) == lax.broadcasted_iota(jnp.int32, (n, n), 1)


def column(row):
    n = row.shape[1]
    return jnp.sum(jnp.where(diagonal(n), jnp.broadcast_to(row, (n, n)), 0.0), axis=1, keepdims=True)


def update(
    mass_scale, sums_ref, mean_ref, var_ref, mass_ref, new_mean_ref, new_var_ref, new_mass_ref
):
    own, width = mean_ref.shape
    mass = column(mass_ref[...])
    counts = jnp.sum(sums_ref[:, 2 * width :], axis=1, keepdims=True)
    kept = 0.4 * mass
    new_mass = kept + 0.6 * mass_scale * counts
    means, variances = mean_ref[...], var_ref[...]
    first = kept * means + 0.6 * mass_scale * sums_ref[:, width : 2 * width]
    second = kept * (variances + means * means) + 0.6 * mass_scale * sums_ref[:, 0:width]
    new_means = first / new_mass
    new_mean_ref[...] = new_means
    new_var_ref[...] = second / new_mass - new_means * new_means
    new_mass_ref[...] = jnp.sum(
        jnp.where(diagonal(own), jnp.broadcast_to(new_mass, (own, own)), 0.0), axis=0, keepdims=True
    )


def kernel(
    n_z, n_comp,
    emb_hbm, mean_ref, var_ref, mass_ref,
    sums_ref,
    emb, wbuf, lhs, offs, xx_hi, xx_lo, st, stats, fac, rt,
    mbuf, sbuf, zbuf, xbuf,
    emb_sem, gs, gr, ss, sr, ms, mr,
):
    f32 = jnp.float32
    rows, width = emb.shape
    own = mean_ref.shape[0]
    part = own // 2
    chunk = 2 * own
    half = n_z * chunk
    tiles = rows // 128
    dp, comp = lax.axis_index("dp"), lax.axis_index("comp")
    z, xh, core = dp // 4, (dp // 2) % 2, dp % 2
    other_x, other_core = 1 - xh, 1 - core

    def at(zz, xx, cc):
        return (zz * 4 + xx * 2 + cc, comp)

    def z_off(k):
        return (z + k + n_z) % n_z

    right, left = at(z_off(1), xh, core), at(z_off(-1), xh, core)
    right2, left2 = at(z_off(2), xh, core), at(z_off(-2), xh, core)
    partner = (z * 4 + other_x * 2 + core, (comp + n_comp // 2) % n_comp)
    sibling = at(z, xh, other_core)

    emb_copy = pltpu.make_async_copy(emb_hbm, emb, emb_sem)
    emb_copy.start()
    barrier = pltpu.get_barrier_semaphore()
    for target in (right, left, right2, left2, partner, sibling):
        pl.semaphore_signal(barrier, inc=1, device_id=target, device_id_type=MESH)

    def greet(t, carry):
        peer = (dp, (comp + t) % n_comp)
        pl.semaphore_signal(barrier, inc=1, device_id=peer, device_id_type=MESH)
        return carry

    lax.fori_loop(1, n_comp, greet, 0)

    means, variances = mean_ref[...], var_ref[...]
    precision = 1.0 / variances
    mean_prec = means * precision
    mass = column(mass_ref[...])
    offset = jnp.log(mass) - 0.5 * jnp.sum(
        jnp.log(variances) + means * mean_prec, axis=1, keepdims=True
    )

    def w_rows(cc, zz, xx):
        return pl.ds(pl.multiple_of(cc * half + zz * chunk + xx * own, own), own)

    mine = w_rows(core, z, xh)
    wbuf[mine, 0:width] = -0.5 * precision
    wbuf[mine, width : 2 * width] = mean_prec
    wbuf[mine, 2 * width :] = jnp.broadcast_to(offset, (own, 128))

    pl.semaphore_wait(barrier, 6 + n_comp - 1)

    cols = (xh, other_x)
    sent = []

    def gather_copy(index, k, c, p, target, n=part):
        start = core * half + z_off(k) * chunk + (cols[c] * own if n < chunk else 0) + p * part
        place = pl.ds(pl.multiple_of(start, part), n)
        return pltpu.make_async_remote_copy(
            src_ref=wbuf.at[place], dst_ref=wbuf.at[place],
            send_sem=gs.at[index], recv_sem=gr.at[index],
            device_id=target, device_id_type=MESH,
        )

    def send(index, k, c, p, target, n=part):
        copy = gather_copy(index, k, c, p, target, n)
        copy.start()
        sent.append(copy)

    def arrived(index, n=part):
        gather_copy(index, 0, 0, 0, partner, n).wait_recv()

    A, B, Q = 0, 1, 2
    item = {A: (0, 0), B: (0, 1), Q: (1, 0)}

    def ring(toward, step, it):
        return (0 if toward > 0 else 10) + ((step - 1) * 3 + it if step < 4 else 9)

    def around(toward, step, it):
        far = step == 4
        target = ((right2 if far else right) if toward > 0 else (left2 if far else left))
        send(ring(toward, step, it), -toward * (2 if far else step - 1), *item[it], target)

    def came(toward, step, it):
        arrived(ring(toward, step, it))

    def x_index(k, p):
        return 20 + {(0, 0): 0, (0, 1): 1, (4, 0): 8, (4, 1): 9}.get((k, p), 1 + 2 * abs(k) - (k < 0))

    def across(k, p):
        send(x_index(k, p), k, 0, p, partner)

    def crossed(k, p):
        arrived(x_index(k, p))

    def to_sibling(k):
        send(30 + k % 8, k, 0, 0, sibling, chunk)

    around(1, 1, A)
    around(-1, 1, B)
    across(0, 0)

    emb_copy.wait()

    def prepare(i, carry):
        place = pl.ds(pl.multiple_of(i * 128, 128), 128)
        x = emb[place, :]
        hi, lo = split(x * x)
        xx_hi[place, 0:width] = hi
        xx_lo[place, 0:width] = lo
        hi, lo = split(x)
        xx_hi[place, width:] = hi
        xx_lo[place, width:] = lo
        return carry

    lax.fori_loop(0, tiles // 2, prepare, 0)
    around(1, 1, B)
    around(-1, 1, A)
    across(0, 1)
    lax.fori_loop(tiles // 2, tiles, prepare, 0)

    groups = ((0, -1, 1), (-2, 2), (-3, 3, 4))
    bases = [2 * chunk * sum(len(g) for g in groups[:i]) for i in range(3)]

    def stage(g):
        n, base = 2 * chunk * len(groups[g]), bases[g]
        places = [(cc, z_off(k)) for cc in (core, other_core) for k in groups[g]]
        for i, (cc, zz) in enumerate(places):
            place = pl.ds(pl.multiple_of(cc * half + zz * chunk, chunk), chunk)
            hi, lo = split(wbuf[place, 0 : 2 * width])
            lhs[i * chunk : (i + 1) * chunk, :] = hi
            lhs[n + i * chunk : n + (i + 1) * chunk, :] = lo
            offs[base + i * chunk : base + (i + 1) * chunk, :] = wbuf[place, 2 * width :]

    block = 256
    blocks = rows // block

    def score(g, first, last):
        n, base = 2 * chunk * len(groups[g]), bases[g]

        def body(b, carry):
            place = pl.ds(pl.multiple_of(b * block, block), block)
            both = lax.dot_general(
                lhs[0 : 2 * n, :], xx_hi[place, :], NT, preferred_element_type=f32
            )
            low = lax.dot_general(lhs[0:n, :], xx_lo[place, :], NT, preferred_element_type=f32)
            off = offs[base : base + n, :]
            st[base : base + n, place] = both[:n] + both[n:] + low + jnp.concatenate([off, off], 1)
            return carry

        lax.fori_loop(first, last, body, 0)

    def sibling_arrived(g):
        for k in groups[g]:
            arrived(30 + k % 8, chunk)

    came(1, 1, A)
    around(1, 2, A)
    came(-1, 1, B)
    around(-1, 2, B)
    across(1, 1)
    crossed(0, 0)
    around(1, 1, Q)
    around(-1, 1, Q)
    came(1, 1, B)
    around(1, 2, B)
    across(-1, 1)
    came(-1, 1, A)
    around(-1, 2, A)
    crossed(0, 1)
    to_sibling(0)
    came(1, 2, A)
    around(1, 4, A)
    around(1, 3, A)
    came(-1, 2, B)
    around(-1, 4, B)
    around(-1, 3, B)
    across(2, 1)
    came(1, 1, Q)
    around(1, 2, Q)
    came(-1, 1, Q)
    around(-1, 2, Q)
    crossed(1, 1)
    to_sibling(1)
    came(1, 2, B)
    around(1, 3, B)
    across(-2, 1)
    came(-1, 2, A)
    around(-1, 3, A)
    crossed(-1, 1)
    to_sibling(-1)
    sibling_arrived(0)
    stage(0)
    score(0, 0, blocks // 2)
    came(1, 2, Q)
    around(1, 3, Q)
    came(-1, 2, Q)
    around(-1, 3, Q)
    came(-1, 3, B)
    across(3, 1)
    crossed(2, 1)
    to_sibling(2)
    came(1, 4, A)
    across(4, 0)
    came(-1, 4, B)
    across(4, 1)
    came(1, 3, B)
    across(-3, 1)
    crossed(-2, 1)
    to_sibling(-2)
    score(0, blocks // 2, blocks)
    sibling_arrived(1)
    stage(1)
    score(1, 0, blocks // 2)
    came(1, 3, A)
    came(-1, 3, A)
    came(1, 3, Q)
    came(-1, 3, Q)
    crossed(3, 1)
    to_sibling(3)
    crossed(-3, 1)
    to_sibling(-3)
    score(1, blocks // 2, blocks)
    crossed(4, 0)
    crossed(4, 1)
    to_sibling(4)
    sibling_arrived(2)
    stage(2)
    score(2, 0, blocks)

    for i in range(tiles):
        lanes = slice(i * 128, (i + 1) * 128)
        s = st[:, lanes]
        peak = jnp.max(s, axis=0, keepdims=True)
        e = jnp.exp(s - peak)
        st[:, lanes] = e
        stats[comp, i : i + 1, :] = peak
        stats[comp, tiles + i : tiles + i + 1, :] = jnp.sum(e, axis=0, keepdims=True)

    def stat_copy(t):
        return pltpu.make_async_remote_copy(
            src_ref=stats.at[comp], dst_ref=stats.at[comp],
            send_sem=ss.at[t], recv_sem=sr.at[t],
            device_id=(dp, (comp + t) % n_comp), device_id_type=MESH,
        )

    def stat_start(t, carry):
        stat_copy(t).start()
        return carry

    def stat_wait(t, carry):
        stat_copy(t).wait_recv()
        return carry

    lax.fori_loop(1, n_comp, stat_start, 0)
    lax.fori_loop(1, n_comp, stat_wait, 0)
    peaks, totals = stats[:, 0:tiles, :], stats[:, tiles:, :]
    peak = jnp.max(peaks, axis=0)
    total = jnp.sum(totals * jnp.exp(peaks - peak[None]), axis=0)
    fac[...] = jnp.exp(stats[comp, 0:tiles, :] - peak) / total

    counts = None
    for i in range(tiles):
        lanes = slice(i * 128, (i + 1) * 128)
        resp = st[:, lanes] * fac[i : i + 1, :]
        counts = resp if counts is None else counts + resp
        hi, lo = split(resp)
        for g, base in zip(groups, bases):
            n = 2 * chunk * len(g)
            rt[2 * base : 2 * base + n, lanes] = hi[base : base + n]
            rt[2 * base + n : 2 * base + 2 * n, lanes] = lo[base : base + n]
    mbuf[:, 2 * width :] = counts

    def moments(g, first, last):
        n, base = 2 * chunk * len(groups[g]), bases[g]

        def body(b, carry):
            lanes = pl.ds(pl.multiple_of(b * block, block), block)
            both = lax.dot_general(
                rt[2 * base : 2 * base + 2 * n, :], xx_hi[:, lanes], NN, preferred_element_type=f32
            )
            low = lax.dot_general(
                rt[2 * base : 2 * base + n, :], xx_lo[:, lanes], NN, preferred_element_type=f32
            )
            mbuf[base : base + n, lanes] = both[:n] + both[n:] + low
            return carry

        lax.fori_loop(first, last, body, 0)

    def reduce_copy(index, src, dst, target):
        return pltpu.make_async_remote_copy(
            src_ref=src, dst_ref=dst, send_sem=ms.at[index], recv_sem=mr.at[index],
            device_id=target, device_id_type=MESH,
        )

    def push(index, src, dst, target):
        copy = reduce_copy(index, src, dst, target)
        copy.start()
        sent.append(copy)

    def landed(index, dst):
        reduce_copy(index, dst, dst, partner).wait_recv()

    lanes_of = (slice(0, width), slice(width, 2 * width + 128))

    def spot(g, i):
        h, base = chunk * len(groups[g]), bases[g]
        return sbuf.at[base // 2 : base // 2 + h, lanes_of[i]]

    def moments_half(g, i):
        h, base, steps = chunk * len(groups[g]), bases[g], 2 * width // block
        moments(g, i * steps // 2, (i + 1) * steps // 2)
        push(30 + 2 * g + i, mbuf.at[base + h : base + 2 * h, lanes_of[i]], spot(g, i), sibling)

    def add_sibling(g):
        h, base = chunk * len(groups[g]), bases[g]
        for i in range(2):
            landed(30 + 2 * g + i, spot(g, i))
            mbuf[base : base + h, lanes_of[i]] += spot(g, i)[...]

    def m_rows(k, c, p):
        g = [i for i in range(3) if k in groups[i]][0]
        start = bases[g] + groups[g].index(k) * chunk + cols[c] * own + p * part
        return pl.ds(pl.multiple_of(start, part), part)

    def give(k, p):
        i = x_index(k, p)
        push(i, mbuf.at[m_rows(k, 1, p)], xbuf.at[i - 20], partner)

    def take(k, p):
        i = x_index(k, p)
        landed(i, xbuf.at[i - 20])
        mbuf[m_rows(k, 0, p), :] += xbuf[i - 20]

    def r_index(toward, step, it):
        return (0 if toward > 0 else 10) + ((step - 2) * 3 + it if step > 1 else 9)

    def begin(toward, step, it):
        i = r_index(toward, step, it)
        if step == 1:
            src, target = mbuf.at[m_rows(4, *item[it])], right2 if toward > 0 else left2
        else:
            src, target = mbuf.at[m_rows(toward * 3, *item[it])], right if toward > 0 else left
        push(i, src, zbuf.at[i], target)

    def extend(toward, step, it):
        i, j = r_index(toward, step - 1, it), r_index(toward, step, it)
        landed(i, zbuf.at[i])
        value = zbuf[i] + mbuf[m_rows(toward * (5 - step), *item[it]), :]
        if step == 3 and it == (A if toward > 0 else B):
            far = r_index(toward, 1, it)
            landed(far, zbuf.at[far])
            value += zbuf[far]
        zbuf[i] = value
        push(j, zbuf.at[i], zbuf.at[j], right if toward > 0 else left)

    def finish(it):
        place = m_rows(0, *item[it])
        value = mbuf[place, :]
        for toward in (1, -1):
            i = r_index(toward, 4, it)
            landed(i, zbuf.at[i])
            value += zbuf[i]
        return value

    moments_half(2, 0)
    moments_half(2, 1)
    moments_half(1, 0)
    add_sibling(2)
    give(4, 0)
    give(4, 1)
    give(3, 1)
    give(-3, 1)
    begin(1, 2, Q)
    begin(-1, 2, Q)
    begin(1, 2, A)
    begin(-1, 2, A)
    moments_half(1, 1)
    add_sibling(1)
    give(2, 1)
    give(-2, 1)
    take(4, 0)
    begin(1, 1, A)
    take(4, 1)
    begin(-1, 1, B)
    take(3, 1)
    begin(1, 2, B)
    take(-3, 1)
    begin(-1, 2, B)
    moments_half(0, 0)
    extend(1, 3, Q)
    extend(-1, 3, Q)
    extend(-1, 3, A)
    take(2, 1)
    take(-2, 1)
    moments_half(0, 1)
    extend(1, 3, B)
    extend(1, 3, A)
    extend(-1, 3, B)
    add_sibling(0)
    give(1, 1)
    give(-1, 1)
    give(0, 1)
    extend(1, 4, Q)
    extend(-1, 4, Q)
    extend(-1, 4, A)
    take(1, 1)
    extend(1, 4, B)
    extend(1, 4, A)
    take(-1, 1)
    extend(-1, 4, B)
    take(0, 1)
    mbuf[m_rows(0, 1, 0), :] = finish(Q)
    give(0, 0)
    sums_ref[part:, :] = finish(B)
    last = finish(A)
    landed(20, xbuf.at[0])
    sums_ref[0:part, :] = last + xbuf[0]

    for copy in sent:
        copy.wait_send()

    def stat_sent(t, carry):
        stat_copy(t).wait_send()
        return carry

    lax.fori_loop(1, n_comp, stat_sent, 0)


def solution(mesh):
    n_dp, n_comp = mesh.shape["dp"], mesh.shape["comp"]
    n_z = n_dp // 4

    def per_device(embeddings, comp_means, comp_variances, comp_mass):
        rows, width = embeddings.shape
        own = comp_means.shape[0]
        group = own * n_dp
        wide = 2 * width + 128
        tiles = rows // 128
        f32, bf16 = jnp.float32, jnp.bfloat16
        vmem, dma = pltpu.VMEM, pltpu.SemaphoreType.DMA
        inside = pl.BlockSpec(memory_space=pltpu.VMEM)
        mass = comp_mass.reshape(1, own)
        sums = pl.pallas_call(
            functools.partial(kernel, n_z, n_comp),
            out_shape=jax.ShapeDtypeStruct((own, wide), f32),
            in_specs=[pl.BlockSpec(memory_space=pl.ANY), inside, inside, inside],
            out_specs=inside,
            scratch_shapes=[
                vmem((rows, width), f32),
                vmem((group, wide), f32),
                vmem((24 * own, 2 * width), bf16),
                vmem((group, 128), f32),
                vmem((rows, 2 * width), bf16),
                vmem((rows, 2 * width), bf16),
                vmem((group, rows), f32),
                vmem((n_comp, 2 * tiles, 128), f32),
                vmem((tiles, 128), f32),
                vmem((2 * group, rows), bf16),
                vmem((group, wide), f32),
                vmem((group // 2, wide), f32),
                vmem((20, own // 2, wide), f32),
                vmem((10, own // 2, wide), f32),
                dma, dma((38,)), dma((38,)), dma((n_comp,)), dma((n_comp,)), dma((36,)), dma((36,)),
            ],
            compiler_params=pltpu.CompilerParams(
                collective_id=0, has_side_effects=True, vmem_limit_bytes=56 * 1024 * 1024
            ),
        )(embeddings, comp_means, comp_variances, mass)
        new_means, new_variances, new_mass = pl.pallas_call(
            functools.partial(update, (group * n_comp) / (rows * n_dp)),
            out_shape=[
                jax.ShapeDtypeStruct((own, width), f32),
                jax.ShapeDtypeStruct((own, width), f32),
                jax.ShapeDtypeStruct((1, own), f32),
            ],
            in_specs=[inside] * 4,
            out_specs=[inside] * 3,
        )(sums, comp_means, comp_variances, mass)
        return new_means, new_variances, new_mass.reshape(own)

    placed = (P("dp", None), P(("comp", "dp"), None), P(("comp", "dp"), None), P(("comp", "dp")))
    return jax.shard_map(
        per_device,
        mesh=mesh,
        in_specs=placed,
        out_specs=(P(("comp", "dp"), None), P(("comp", "dp"), None), P(("comp", "dp"))),
        check_vma=False,
    )
```

```python
import functools

import jax
import jax.numpy as jnp
from jax import lax
from jax.experimental import pallas as pl
from jax.experimental.pallas import tpu as pltpu
from jax.sharding import PartitionSpec as P

MESH = pl.DeviceIdType.MESH
NT = (((1,), (1,)), ((), ()))
NN = (((1,), (0,)), ((), ()))


def split(value):
    high = value.astype(jnp.bfloat16)
    return high, (value - high.astype(jnp.float32)).astype(jnp.bfloat16)


def diagonal(n):
    return lax.broadcasted_iota(jnp.int32, (n, n), 0) == lax.broadcasted_iota(jnp.int32, (n, n), 1)


def column(row):
    n = row.shape[1]
    return jnp.sum(jnp.where(diagonal(n), jnp.broadcast_to(row, (n, n)), 0.0), axis=1, keepdims=True)


def update(
    mass_scale, sums_ref, mean_ref, var_ref, mass_ref, new_mean_ref, new_var_ref, new_mass_ref
):
    own, width = mean_ref.shape
    mass = column(mass_ref[...])
    counts = jnp.sum(sums_ref[:, 2 * width :], axis=1, keepdims=True)
    kept = 0.4 * mass
    new_mass = kept + 0.6 * mass_scale * counts
    means, variances = mean_ref[...], var_ref[...]
    first = kept * means + 0.6 * mass_scale * sums_ref[:, width : 2 * width]
    second = kept * (variances + means * means) + 0.6 * mass_scale * sums_ref[:, 0:width]
    new_means = first / new_mass
    new_mean_ref[...] = new_means
    new_var_ref[...] = second / new_mass - new_means * new_means
    new_mass_ref[...] = jnp.sum(
        jnp.where(diagonal(own), jnp.broadcast_to(new_mass, (own, own)), 0.0), axis=0, keepdims=True
    )


def kernel(
    n_z, n_comp,
    emb_hbm, mean_ref, var_ref, mass_ref,
    sums_ref,
    emb, wbuf, lhs, offs, xx_hi, xx_lo, st, stats, fac, rt,
    mbuf, sbuf, zbuf, xbuf,
    emb_sem, gs, gr, ss, sr, ms, mr,
):
    f32 = jnp.float32
    rows, width = emb.shape
    own = mean_ref.shape[0]
    part = own // 2
    chunk = 2 * own
    half = n_z * chunk
    tiles = rows // 128
    dp, comp = lax.axis_index("dp"), lax.axis_index("comp")
    z, xh, core = dp // 4, (dp // 2) % 2, dp % 2
    other_x, other_core = 1 - xh, 1 - core

    def at(zz, xx, cc):
        return (zz * 4 + xx * 2 + cc, comp)

    def z_off(k):
        return (z + k + n_z) % n_z

    right, left = at(z_off(1), xh, core), at(z_off(-1), xh, core)
    right2, left2 = at(z_off(2), xh, core), at(z_off(-2), xh, core)
    partner = (z * 4 + other_x * 2 + core, (comp + n_comp // 2) % n_comp)
    sibling = at(z, xh, other_core)

    emb_copy = pltpu.make_async_copy(emb_hbm, emb, emb_sem)
    emb_copy.start()
    barrier = pltpu.get_barrier_semaphore()
    for target in (right, left, right2, left2, partner, sibling):
        pl.semaphore_signal(barrier, inc=1, device_id=target, device_id_type=MESH)

    def greet(t, carry):
        peer = (dp, (comp + t) % n_comp)
        pl.semaphore_signal(barrier, inc=1, device_id=peer, device_id_type=MESH)
        return carry

    lax.fori_loop(1, n_comp, greet, 0)

    means, variances = mean_ref[...], var_ref[...]
    precision = 1.0 / variances
    mean_prec = means * precision
    mass = column(mass_ref[...])
    offset = jnp.log(mass) - 0.5 * jnp.sum(
        jnp.log(variances) + means * mean_prec, axis=1, keepdims=True
    )

    def w_rows(cc, zz, xx):
        return pl.ds(pl.multiple_of(cc * half + zz * chunk + xx * own, own), own)

    mine = w_rows(core, z, xh)
    wbuf[mine, 0:width] = -0.5 * precision
    wbuf[mine, width : 2 * width] = mean_prec
    wbuf[mine, 2 * width :] = jnp.broadcast_to(offset, (own, 128))

    pl.semaphore_wait(barrier, 6 + n_comp - 1)

    cols = (xh, other_x)
    sent = []

    def gather_copy(index, k, c, p, target, n=part):
        start = core * half + z_off(k) * chunk + (cols[c] * own if n < chunk else 0) + p * part
        place = pl.ds(pl.multiple_of(start, part), n)
        return pltpu.make_async_remote_copy(
            src_ref=wbuf.at[place], dst_ref=wbuf.at[place],
            send_sem=gs.at[index], recv_sem=gr.at[index],
            device_id=target, device_id_type=MESH,
        )

    def send(index, k, c, p, target, n=part):
        copy = gather_copy(index, k, c, p, target, n)
        copy.start()
        sent.append(copy)

    def arrived(index, n=part):
        gather_copy(index, 0, 0, 0, partner, n).wait_recv()

    A, B, Q, S = 0, 1, 2, 3
    item = {A: (0, 0), B: (0, 1), Q: (1, 0), S: (1, 1)}

    def ring(toward, step, it):
        if it == S:
            return 38 if toward > 0 else 39
        return (0 if toward > 0 else 10) + ((step - 1) * 3 + it if step < 4 else 9)

    def around(toward, step, it):
        far = step == 4
        target = ((right2 if far else right) if toward > 0 else (left2 if far else left))
        send(ring(toward, step, it), -toward * (2 if far else step - 1), *item[it], target)

    def came(toward, step, it):
        arrived(ring(toward, step, it))

    def x_index(k, p):
        return 20 + {(0, 0): 0, (0, 1): 1, (4, 0): 8, (4, 1): 9}.get((k, p), 1 + 2 * abs(k) - (k < 0))

    def across(k, p):
        send(x_index(k, p), k, 0, p, partner)

    def crossed(k, p):
        arrived(x_index(k, p))

    def to_sibling(k):
        send(30 + k % 8, k, 0, 0, sibling, chunk)

    around(1, 1, A)
    around(-1, 1, B)
    across(0, 0)

    emb_copy.wait()

    def prepare(i, carry):
        place = pl.ds(pl.multiple_of(i * 128, 128), 128)
        x = emb[place, :]
        hi, lo = split(x * x)
        xx_hi[place, 0:width] = hi
        xx_lo[place, 0:width] = lo
        hi, lo = split(x)
        xx_hi[place, width:] = hi
        xx_lo[place, width:] = lo
        return carry

    lax.fori_loop(0, tiles // 2, prepare, 0)
    around(1, 1, B)
    around(-1, 1, A)
    across(0, 1)
    lax.fori_loop(tiles // 2, tiles, prepare, 0)

    groups = ((0, -1, 1), (-2, 2), (-3, 3, 4))
    bases = [2 * chunk * sum(len(g) for g in groups[:i]) for i in range(3)]

    def stage(g):
        n, base = 2 * chunk * len(groups[g]), bases[g]
        places = [(cc, z_off(k)) for cc in (core, other_core) for k in groups[g]]
        for i, (cc, zz) in enumerate(places):
            place = pl.ds(pl.multiple_of(cc * half + zz * chunk, chunk), chunk)
            hi, lo = split(wbuf[place, 0 : 2 * width])
            lhs[i * chunk : (i + 1) * chunk, :] = hi
            lhs[n + i * chunk : n + (i + 1) * chunk, :] = lo
            offs[base + i * chunk : base + (i + 1) * chunk, :] = wbuf[place, 2 * width :]

    def score(g, first, last, block):
        n, base = 2 * chunk * len(groups[g]), bases[g]
        for b in range(first, last, block):
            place = slice(b, b + block)
            both = lax.dot_general(
                lhs[0 : 2 * n, :], xx_hi[place, :], NT, preferred_element_type=f32
            )
            low = lax.dot_general(lhs[0:n, :], xx_lo[place, :], NT, preferred_element_type=f32)
            off = jnp.concatenate([offs[base : base + n, :]] * (block // 128), 1)
            st[base : base + n, place] = both[:n] + both[n:] + low + off

    def sibling_arrived(g):
        for k in groups[g]:
            arrived(30 + k % 8, chunk)

    came(1, 1, A)
    around(1, 2, A)
    came(-1, 1, B)
    around(-1, 2, B)
    across(1, 1)
    crossed(0, 0)
    around(1, 1, Q)
    around(-1, 1, Q)
    came(1, 1, B)
    around(1, 2, B)
    across(-1, 1)
    came(-1, 1, A)
    around(-1, 2, A)
    crossed(0, 1)
    to_sibling(0)
    came(1, 2, A)
    around(1, 4, A)
    came(-1, 2, B)
    around(-1, 4, B)
    across(2, 1)
    came(1, 1, Q)
    around(1, 2, Q)
    came(-1, 1, Q)
    around(-1, 2, Q)
    crossed(1, 1)
    to_sibling(1)
    came(1, 2, B)
    across(-2, 1)
    came(-1, 2, A)
    around(1, 3, A)
    around(-1, 3, B)
    around(1, 3, B)
    around(-1, 3, A)
    crossed(-1, 1)
    to_sibling(-1)
    sibling_arrived(0)
    stage(0)
    score(0, 0, rows // 2, rows // 2)
    came(1, 2, Q)
    around(1, 3, Q)
    came(-1, 2, Q)
    around(-1, 3, Q)
    came(-1, 3, B)
    crossed(2, 1)
    around(-1, 3, S)
    to_sibling(2)
    came(1, 4, A)
    across(4, 0)
    came(-1, 4, B)
    across(4, 1)
    came(1, 3, B)
    crossed(-2, 1)
    around(1, 3, S)
    to_sibling(-2)
    score(0, rows // 2, rows, rows // 2)
    sibling_arrived(1)
    stage(1)
    score(1, 0, rows // 2, rows // 2)
    came(1, 3, A)
    came(-1, 3, A)
    came(1, 3, Q)
    came(-1, 3, Q)
    came(-1, 3, S)
    to_sibling(3)
    came(1, 3, S)
    to_sibling(-3)
    score(1, rows // 2, rows, rows // 2)
    crossed(4, 0)
    crossed(4, 1)
    to_sibling(4)
    sibling_arrived(2)
    stage(2)
    score(2, 0, rows, rows)

    for i in range(tiles):
        lanes = slice(i * 128, (i + 1) * 128)
        s = st[:, lanes]
        peak = jnp.max(s, axis=0, keepdims=True)
        e = jnp.exp(s - peak)
        st[:, lanes] = e
        fac[i : i + 1, :] = peak
        stats[comp, i : i + 1, :] = peak + jnp.log(jnp.sum(e, axis=0, keepdims=True))

    def stat_copy(t):
        return pltpu.make_async_remote_copy(
            src_ref=stats.at[comp], dst_ref=stats.at[comp],
            send_sem=ss.at[t], recv_sem=sr.at[t],
            device_id=(dp, (comp + t) % n_comp), device_id_type=MESH,
        )

    def stat_start(t, carry):
        stat_copy(t).start()
        return carry

    def stat_wait(t, carry):
        stat_copy(t).wait_recv()
        return carry

    lax.fori_loop(1, n_comp, stat_start, 0)
    lax.fori_loop(1, n_comp, stat_wait, 0)
    logs = stats[...]
    peak = jnp.max(logs, axis=0)
    total = jnp.sum(jnp.exp(logs - peak[None]), axis=0)
    fac[...] = jnp.exp(fac[...] - peak) / total

    counts = None
    for i in range(tiles):
        lanes = slice(i * 128, (i + 1) * 128)
        resp = st[:, lanes] * fac[i : i + 1, :]
        counts = resp if counts is None else counts + resp
        hi, lo = split(resp)
        for g, base in zip(groups, bases):
            n = 2 * chunk * len(g)
            rt[2 * base : 2 * base + n, lanes] = hi[base : base + n]
            rt[2 * base + n : 2 * base + 2 * n, lanes] = lo[base : base + n]
    mbuf[:, 2 * width :] = counts

    def moments(g, lanes):
        n, base = 2 * chunk * len(groups[g]), bases[g]
        both = lax.dot_general(
            rt[2 * base : 2 * base + 2 * n, :], xx_hi[:, lanes], NN, preferred_element_type=f32
        )
        low = lax.dot_general(
            rt[2 * base : 2 * base + n, :], xx_lo[:, lanes], NN, preferred_element_type=f32
        )
        mbuf[base : base + n, lanes] = both[:n] + both[n:] + low

    def reduce_copy(index, src, dst, target):
        return pltpu.make_async_remote_copy(
            src_ref=src, dst_ref=dst, send_sem=ms.at[index], recv_sem=mr.at[index],
            device_id=target, device_id_type=MESH,
        )

    def push(index, src, dst, target):
        copy = reduce_copy(index, src, dst, target)
        copy.start()
        sent.append(copy)

    def landed(index, dst):
        reduce_copy(index, dst, dst, partner).wait_recv()

    lanes_of = (slice(0, width), slice(width, 2 * width + 128))

    def spot(g, i):
        h, base = chunk * len(groups[g]), bases[g]
        return sbuf.at[base // 2 : base // 2 + h, lanes_of[i]]

    def moments_half(g, i):
        h, base = chunk * len(groups[g]), bases[g]
        moments(g, slice(i * width, (i + 1) * width))
        push(30 + 2 * g + i, mbuf.at[base + h : base + 2 * h, lanes_of[i]], spot(g, i), sibling)

    def add_sibling(g):
        h, base = chunk * len(groups[g]), bases[g]
        for i in range(2):
            landed(30 + 2 * g + i, spot(g, i))
            mbuf[base : base + h, lanes_of[i]] += spot(g, i)[...]

    def m_rows(k, c, p):
        g = [i for i in range(3) if k in groups[i]][0]
        start = bases[g] + groups[g].index(k) * chunk + cols[c] * own + p * part
        return pl.ds(pl.multiple_of(start, part), part)

    def give(k, p):
        i = x_index(k, p)
        push(i, mbuf.at[m_rows(k, 1, p)], xbuf.at[i - 20], partner)

    def take(k, p):
        i = x_index(k, p)
        landed(i, xbuf.at[i - 20])
        mbuf[m_rows(k, 0, p), :] += xbuf[i - 20]

    def r_index(toward, step, it):
        if it == S:
            return 38 if toward > 0 else 39
        return (0 if toward > 0 else 10) + ((step - 2) * 3 + it if step > 1 else 9)

    def begin(toward, step, it):
        i = r_index(toward, step, it)
        if step == 1:
            src, target = mbuf.at[m_rows(4, *item[it])], right2 if toward > 0 else left2
        else:
            src, target = mbuf.at[m_rows(toward * 3, *item[it])], right if toward > 0 else left
        push(i, src, zbuf.at[i if it < S else i - 18], target)

    def extend(toward, step, it):
        i, j = r_index(toward, step - 1, it), r_index(toward, step, it)
        landed(i, zbuf.at[i])
        value = zbuf[i] + mbuf[m_rows(toward * (5 - step), *item[it]), :]
        if step == 3 and it == (A if toward > 0 else B):
            far = r_index(toward, 1, it)
            landed(far, zbuf.at[far])
            value += zbuf[far]
        zbuf[i] = value
        push(j, zbuf.at[i], zbuf.at[j], right if toward > 0 else left)

    def merge(toward):
        i = r_index(toward, 2, S)
        landed(i, zbuf.at[i - 18])
        mbuf[m_rows(2 * toward, 1, 1), :] += zbuf[i - 18]

    def finish(it):
        place = m_rows(0, *item[it])
        value = mbuf[place, :]
        for toward in (1, -1):
            i = r_index(toward, 4, it)
            landed(i, zbuf.at[i])
            value += zbuf[i]
        return value

    moments_half(2, 0)
    moments_half(2, 1)
    moments_half(1, 0)
    add_sibling(2)
    give(4, 0)
    give(4, 1)
    begin(1, 2, S)
    begin(-1, 2, S)
    begin(1, 2, Q)
    begin(-1, 2, Q)
    moments_half(1, 1)
    begin(1, 2, B)
    begin(-1, 2, A)
    begin(1, 2, A)
    begin(-1, 2, B)
    moments_half(0, 0)
    add_sibling(1)
    merge(1)
    give(2, 1)
    merge(-1)
    give(-2, 1)
    take(4, 0)
    begin(1, 1, A)
    take(4, 1)
    begin(-1, 1, B)
    extend(1, 3, Q)
    extend(-1, 3, Q)
    moments_half(0, 1)
    extend(-1, 3, A)
    add_sibling(0)
    give(1, 1)
    give(-1, 1)
    give(0, 1)
    take(2, 1)
    extend(1, 3, B)
    extend(1, 4, Q)
    extend(-1, 4, Q)
    extend(1, 3, A)
    take(-2, 1)
    extend(-1, 3, B)
    extend(-1, 4, A)
    take(1, 1)
    extend(1, 4, B)
    mbuf[m_rows(0, 1, 0), :] = finish(Q)
    give(0, 0)
    extend(1, 4, A)
    take(-1, 1)
    extend(-1, 4, B)
    take(0, 1)
    sums_ref[part:, :] = finish(B)
    last = finish(A)
    landed(20, xbuf.at[0])
    sums_ref[0:part, :] = last + xbuf[0]

    for copy in sent:
        copy.wait_send()

    def stat_sent(t, carry):
        stat_copy(t).wait_send()
        return carry

    lax.fori_loop(1, n_comp, stat_sent, 0)


def solution(mesh):
    n_dp, n_comp = mesh.shape["dp"], mesh.shape["comp"]
    n_z = n_dp // 4

    def per_device(embeddings, comp_means, comp_variances, comp_mass):
        rows, width = embeddings.shape
        own = comp_means.shape[0]
        group = own * n_dp
        wide = 2 * width + 128
        tiles = rows // 128
        f32, bf16 = jnp.float32, jnp.bfloat16
        vmem, dma = pltpu.VMEM, pltpu.SemaphoreType.DMA
        inside = pl.BlockSpec(memory_space=pltpu.VMEM)
        mass = comp_mass.reshape(1, own)
        sums = pl.pallas_call(
            functools.partial(kernel, n_z, n_comp),
            out_shape=jax.ShapeDtypeStruct((own, wide), f32),
            in_specs=[pl.BlockSpec(memory_space=pl.ANY), inside, inside, inside],
            out_specs=inside,
            scratch_shapes=[
                vmem((rows, width), f32),
                vmem((group, wide), f32),
                vmem((24 * own, 2 * width), bf16),
                vmem((group, 128), f32),
                vmem((rows, 2 * width), bf16),
                vmem((rows, 2 * width), bf16),
                vmem((group, rows), f32),
                vmem((n_comp, tiles, 128), f32),
                vmem((tiles, 128), f32),
                vmem((2 * group, rows), bf16),
                vmem((group, wide), f32),
                vmem((group // 2, wide), f32),
                vmem((22, own // 2, wide), f32),
                vmem((10, own // 2, wide), f32),
                dma, dma((40,)), dma((40,)), dma((n_comp,)), dma((n_comp,)), dma((40,)), dma((40,)),
            ],
            compiler_params=pltpu.CompilerParams(
                collective_id=0, has_side_effects=True, vmem_limit_bytes=56 * 1024 * 1024
            ),
        )(embeddings, comp_means, comp_variances, mass)
        new_means, new_variances, new_mass = pl.pallas_call(
            functools.partial(update, (group * n_comp) / (rows * n_dp)),
            out_shape=[
                jax.ShapeDtypeStruct((own, width), f32),
                jax.ShapeDtypeStruct((own, width), f32),
                jax.ShapeDtypeStruct((1, own), f32),
            ],
            in_specs=[inside] * 4,
            out_specs=[inside] * 3,
        )(sums, comp_means, comp_variances, mass)
        return new_means, new_variances, new_mass.reshape(own)

    placed = (P("dp", None), P(("comp", "dp"), None), P(("comp", "dp"), None), P(("comp", "dp")))
    return jax.shard_map(
        per_device,
        mesh=mesh,
        in_specs=placed,
        out_specs=(P(("comp", "dp"), None), P(("comp", "dp"), None), P(("comp", "dp"))),
        check_vma=False,
    )
```

```python
import functools

import jax
import jax.numpy as jnp
from jax import lax
from jax.experimental import pallas as pl
from jax.experimental.pallas import tpu as pltpu
from jax.sharding import PartitionSpec as P

MESH = pl.DeviceIdType.MESH
NT = (((1,), (1,)), ((), ()))
NN = (((1,), (0,)), ((), ()))


def split(value):
    high = value.astype(jnp.bfloat16)
    return high, (value - high.astype(jnp.float32)).astype(jnp.bfloat16)


def diagonal(n):
    return lax.broadcasted_iota(jnp.int32, (n, n), 0) == lax.broadcasted_iota(jnp.int32, (n, n), 1)


def column(row):
    n = row.shape[1]
    return jnp.sum(jnp.where(diagonal(n), jnp.broadcast_to(row, (n, n)), 0.0), axis=1, keepdims=True)


def update(
    mass_scale, sums_ref, mean_ref, var_ref, mass_ref, new_mean_ref, new_var_ref, new_mass_ref
):
    own, width = mean_ref.shape
    mass = column(mass_ref[...])
    part = own // 2
    tile = sums_ref[part:, 2 * width :]
    low_lanes = lax.broadcasted_iota(jnp.int32, tile.shape, 1) < 64
    counts = jnp.concatenate(
        [
            jnp.sum(jnp.where(low_lanes, tile, 0.0), axis=1, keepdims=True),
            jnp.sum(jnp.where(low_lanes, 0.0, tile), axis=1, keepdims=True),
        ]
    )
    kept = 0.4 * mass
    new_mass = kept + 0.6 * mass_scale * counts
    means, variances = mean_ref[...], var_ref[...]
    first = kept * means + 0.6 * mass_scale * sums_ref[:, width : 2 * width]
    second = kept * (variances + means * means) + 0.6 * mass_scale * sums_ref[:, 0:width]
    new_means = first / new_mass
    new_mean_ref[...] = new_means
    new_var_ref[...] = second / new_mass - new_means * new_means
    new_mass_ref[...] = jnp.sum(
        jnp.where(diagonal(own), jnp.broadcast_to(new_mass, (own, own)), 0.0), axis=0, keepdims=True
    )


def kernel(
    n_z, n_comp,
    emb_hbm, mean_ref, var_ref, mass_ref,
    sums_ref,
    emb, wbuf, lhs, offs, xx_hi, xx_lo, st, stats, fac, rt,
    mbuf, sbuf, zbuf, xbuf,
    emb_sem, gs, gr, ss, sr, ms, mr,
):
    f32 = jnp.float32
    rows, width = emb.shape
    own = mean_ref.shape[0]
    part = own // 2
    chunk = 2 * own
    half = n_z * chunk
    tiles = rows // 128
    dp, comp = lax.axis_index("dp"), lax.axis_index("comp")
    z, xh, core = dp // 4, (dp // 2) % 2, dp % 2
    other_x, other_core = 1 - xh, 1 - core

    def at(zz, xx, cc):
        return (zz * 4 + xx * 2 + cc, comp)

    def z_off(k):
        return (z + k + n_z) % n_z

    right, left = at(z_off(1), xh, core), at(z_off(-1), xh, core)
    right2, left2 = at(z_off(2), xh, core), at(z_off(-2), xh, core)
    partner = (z * 4 + other_x * 2 + core, (comp + n_comp // 2) % n_comp)
    sibling = at(z, xh, other_core)

    emb_copy = pltpu.make_async_copy(emb_hbm, emb, emb_sem)
    emb_copy.start()
    barrier = pltpu.get_barrier_semaphore()
    for target in (right, left, right2, left2, partner, sibling):
        pl.semaphore_signal(barrier, inc=1, device_id=target, device_id_type=MESH)

    def greet(t, carry):
        peer = (dp, (comp + t) % n_comp)
        pl.semaphore_signal(barrier, inc=1, device_id=peer, device_id_type=MESH)
        return carry

    lax.fori_loop(1, n_comp, greet, 0)

    means, variances = mean_ref[...], var_ref[...]
    precision = 1.0 / variances
    mean_prec = means * precision
    mass = column(mass_ref[...])
    offset = jnp.log(mass) - 0.5 * jnp.sum(
        jnp.log(variances) + means * mean_prec, axis=1, keepdims=True
    )

    def w_rows(cc, zz, xx):
        return pl.ds(pl.multiple_of(cc * half + zz * chunk + xx * own, own), own)

    mine = w_rows(core, z, xh)
    wbuf[mine, 0:width] = -0.5 * precision
    wbuf[mine, width : 2 * width] = mean_prec
    low_lanes = lax.broadcasted_iota(jnp.int32, (part, 128), 1) < 64
    second = pl.ds(pl.multiple_of(core * half + z * chunk + xh * own + part, part), part)
    wbuf[second, 2 * width :] = jnp.where(
        low_lanes,
        jnp.broadcast_to(offset[0:part], (part, 128)),
        jnp.broadcast_to(offset[part:own], (part, 128)),
    )

    pl.semaphore_wait(barrier, 6 + n_comp - 1)

    cols = (xh, other_x)
    sent = []

    def gather_copy(index, k, c, p, target, n=part):
        start = core * half + z_off(k) * chunk + (cols[c] * own if n < chunk else 0) + p * part
        place = pl.ds(pl.multiple_of(start, part), n)
        span = slice(0, 2 * width) if n == part and p == 0 else slice(0, 2 * width + 128)
        return pltpu.make_async_remote_copy(
            src_ref=wbuf.at[place, span], dst_ref=wbuf.at[place, span],
            send_sem=gs.at[index], recv_sem=gr.at[index],
            device_id=target, device_id_type=MESH,
        )

    def send(index, k, c, p, target, n=part):
        copy = gather_copy(index, k, c, p, target, n)
        copy.start()
        sent.append(copy)

    def arrived(index, p, n=part):
        gather_copy(index, 0, 0, p, partner, n).wait_recv()

    A, B, Q, S = 0, 1, 2, 3
    item = {A: (0, 0), B: (0, 1), Q: (1, 0), S: (1, 1)}

    def ring(toward, step, it):
        if it == S:
            return 38 if toward > 0 else 39
        return (0 if toward > 0 else 10) + ((step - 1) * 3 + it if step < 4 else 9)

    def around(toward, step, it):
        far = step == 4
        target = ((right2 if far else right) if toward > 0 else (left2 if far else left))
        send(ring(toward, step, it), -toward * (2 if far else step - 1), *item[it], target)

    def came(toward, step, it):
        arrived(ring(toward, step, it), item[it][1])

    def x_index(k, p):
        return 20 + {(0, 0): 0, (0, 1): 1, (4, 0): 8, (4, 1): 9}.get((k, p), 1 + 2 * abs(k) - (k < 0))

    def across(k, p):
        send(x_index(k, p), k, 0, p, partner)

    def crossed(k, p):
        arrived(x_index(k, p), p)

    def to_sibling(k):
        send(30 + k % 8, k, 0, 0, sibling, chunk)

    around(1, 1, A)
    around(-1, 1, B)
    across(0, 0)

    emb_copy.wait()

    def prepare(i, carry):
        place = pl.ds(pl.multiple_of(i * 128, 128), 128)
        x = emb[place, :]
        hi, lo = split(x * x)
        xx_hi[place, 0:width] = hi
        xx_lo[place, 0:width] = lo
        hi, lo = split(x)
        xx_hi[place, width:] = hi
        xx_lo[place, width:] = lo
        return carry

    lax.fori_loop(0, tiles // 2, prepare, 0)
    around(1, 1, B)
    around(-1, 1, A)
    across(0, 1)
    lax.fori_loop(tiles // 2, tiles, prepare, 0)

    groups = ((0, -1, 1), (-2, 2), (-3, 3, 4))
    bases = [2 * chunk * sum(len(g) for g in groups[:i]) for i in range(3)]

    def stage(g):
        n, base = 2 * chunk * len(groups[g]), bases[g]
        places = [(cc, z_off(k)) for cc in (core, other_core) for k in groups[g]]
        for i, (cc, zz) in enumerate(places):
            place = pl.ds(pl.multiple_of(cc * half + zz * chunk, chunk), chunk)
            hi, lo = split(wbuf[place, 0 : 2 * width])
            lhs[i * chunk : (i + 1) * chunk, :] = hi
            lhs[n + i * chunk : n + (i + 1) * chunk, :] = lo
            tile = wbuf[place, 2 * width :]
            for r in range(0, chunk, part):
                both = tile[r // own * own + part : r // own * own + own]
                lane = 64 * (r % own // part)
                offs[base + i * chunk + r : base + i * chunk + r + part, :] = jnp.broadcast_to(
                    both[:, lane : lane + 1], (part, 128)
                )

    def score(g, first, last, block):
        n, base = 2 * chunk * len(groups[g]), bases[g]
        for b in range(first, last, block):
            place = slice(b, b + block)
            both = lax.dot_general(
                lhs[0 : 2 * n, :], xx_hi[place, :], NT, preferred_element_type=f32
            )
            low = lax.dot_general(lhs[0:n, :], xx_lo[place, :], NT, preferred_element_type=f32)
            off = jnp.concatenate([offs[base : base + n, :]] * (block // 128), 1)
            st[base : base + n, place] = both[:n] + both[n:] + low + off

    def sibling_arrived(g):
        for k in groups[g]:
            arrived(30 + k % 8, 0, chunk)

    came(1, 1, A)
    around(1, 2, A)
    came(-1, 1, B)
    around(-1, 2, B)
    across(1, 1)
    crossed(0, 0)
    around(1, 1, Q)
    around(-1, 1, Q)
    came(1, 1, B)
    around(1, 2, B)
    across(-1, 1)
    came(-1, 1, A)
    around(-1, 2, A)
    crossed(0, 1)
    to_sibling(0)
    came(1, 2, A)
    around(1, 4, A)
    came(-1, 2, B)
    around(-1, 4, B)
    across(2, 1)
    came(1, 1, Q)
    around(1, 2, Q)
    came(-1, 1, Q)
    around(-1, 2, Q)
    crossed(1, 1)
    to_sibling(1)
    came(1, 2, B)
    across(-2, 1)
    came(-1, 2, A)
    around(1, 3, A)
    around(-1, 3, B)
    around(1, 3, B)
    around(-1, 3, A)
    crossed(-1, 1)
    to_sibling(-1)
    sibling_arrived(0)
    stage(0)
    score(0, 0, rows // 2, rows // 2)
    came(1, 2, Q)
    around(1, 3, Q)
    came(-1, 2, Q)
    around(-1, 3, Q)
    came(-1, 3, B)
    crossed(2, 1)
    around(-1, 3, S)
    to_sibling(2)
    came(1, 4, A)
    across(4, 0)
    came(-1, 4, B)
    across(4, 1)
    came(1, 3, B)
    crossed(-2, 1)
    around(1, 3, S)
    to_sibling(-2)
    score(0, rows // 2, rows, rows // 2)
    sibling_arrived(1)
    stage(1)
    score(1, 0, rows // 2, rows // 2)
    came(1, 3, A)
    came(-1, 3, A)
    came(1, 3, Q)
    came(-1, 3, Q)
    came(-1, 3, S)
    to_sibling(3)
    came(1, 3, S)
    to_sibling(-3)
    score(1, rows // 2, rows, rows // 2)
    crossed(4, 0)
    crossed(4, 1)
    to_sibling(4)
    sibling_arrived(2)
    stage(2)

    def statistic(h):
        for j in range(tiles // 2):
            i = h * tiles // 2 + j
            lanes = slice(i * 128, (i + 1) * 128)
            s = st[:, lanes]
            peak = jnp.max(s, axis=0, keepdims=True)
            e = jnp.exp(s - peak)
            st[:, lanes] = e
            fac[i : i + 1, :] = peak
            stats[h, comp, j : j + 1, :] = peak + jnp.log(jnp.sum(e, axis=0, keepdims=True))

    def stat_copy(h, t):
        return pltpu.make_async_remote_copy(
            src_ref=stats.at[h, comp], dst_ref=stats.at[h, comp],
            send_sem=ss.at[h, t], recv_sem=sr.at[h, t],
            device_id=(dp, (comp + t) % n_comp), device_id_type=MESH,
        )

    def stat_start(h):
        def body(t, carry):
            stat_copy(h, t).start()
            return carry

        lax.fori_loop(1, n_comp, body, 0)

    def responsibilities(h, counts):
        def body(t, carry):
            stat_copy(h, t).wait_recv()
            return carry

        lax.fori_loop(1, n_comp, body, 0)
        logs = stats[h]
        peak = jnp.max(logs, axis=0)
        total = jnp.sum(jnp.exp(logs - peak[None]), axis=0)
        mine = slice(h * tiles // 2, (h + 1) * tiles // 2)
        fac[mine, :] = jnp.exp(fac[mine, :] - peak) / total
        for i in range(h * tiles // 2, (h + 1) * tiles // 2):
            lanes = slice(i * 128, (i + 1) * 128)
            resp = st[:, lanes] * fac[i : i + 1, :]
            counts = resp if counts is None else counts + resp
            hi, lo = split(resp)
            for g, base in zip(groups, bases):
                n = 2 * chunk * len(g)
                rt[2 * base : 2 * base + n, lanes] = hi[base : base + n]
                rt[2 * base + n : 2 * base + 2 * n, lanes] = lo[base : base + n]
        return counts

    score(2, 0, rows // 2, rows // 2)
    statistic(0)
    stat_start(0)
    score(2, rows // 2, rows, rows // 2)
    statistic(1)
    stat_start(1)

    def moments(g, lanes, over=slice(None), add=False):
        n, base = 2 * chunk * len(groups[g]), bases[g]
        both = lax.dot_general(
            rt[2 * base : 2 * base + 2 * n, over], xx_hi[over, lanes], NN, preferred_element_type=f32
        )
        low = lax.dot_general(
            rt[2 * base : 2 * base + n, over], xx_lo[over, lanes], NN, preferred_element_type=f32
        )
        value = both[:n] + both[n:] + low
        mbuf[base : base + n, lanes] = mbuf[base : base + n, lanes] + value if add else value

    def reduce_copy(index, src, dst, target):
        return pltpu.make_async_remote_copy(
            src_ref=src, dst_ref=dst, send_sem=ms.at[index], recv_sem=mr.at[index],
            device_id=target, device_id_type=MESH,
        )

    def push(index, src, dst, target):
        copy = reduce_copy(index, src, dst, target)
        copy.start()
        sent.append(copy)

    def landed(index, dst):
        reduce_copy(index, dst, dst, partner).wait_recv()

    lanes_of = (slice(0, width), slice(width, 2 * width + 128))

    def spot(g, i):
        h, base = chunk * len(groups[g]), bases[g]
        return sbuf.at[base // 2 : base // 2 + h, lanes_of[i]]

    def moments_half(g, i):
        h, base = chunk * len(groups[g]), bases[g]
        lanes = slice(i * width, (i + 1) * width)
        if g == 2:
            moments(g, lanes, slice(rows // 2, rows), True)
        else:
            moments(g, lanes)
        push(30 + 2 * g + i, mbuf.at[base + h : base + 2 * h, lanes_of[i]], spot(g, i), sibling)

    def add_sibling(g):
        h, base = chunk * len(groups[g]), bases[g]
        for i in range(2):
            landed(30 + 2 * g + i, spot(g, i))
            mbuf[base : base + h, lanes_of[i]] += spot(g, i)[...]

    def span(p):
        return slice(0, 2 * width + (128 if p else 0))

    def z_slot(toward, step, it):
        i = r_index(toward, step, it)
        return zbuf.at[i if it < S else i - 18, :, span(item[it][1])]

    def m_rows(k, c, p):
        g = [i for i in range(3) if k in groups[i]][0]
        start = bases[g] + groups[g].index(k) * chunk + cols[c] * own + p * part
        return pl.ds(pl.multiple_of(start, part), part)

    def m_part(k, c, p):
        return mbuf.at[m_rows(k, c, p), span(p)]

    def give(k, p):
        i = x_index(k, p)
        push(i, m_part(k, 1, p), xbuf.at[i - 20, :, span(p)], partner)

    def take(k, p):
        i = x_index(k, p)
        here = xbuf.at[i - 20, :, span(p)]
        landed(i, here)
        m_part(k, 0, p)[...] += here[...]

    def r_index(toward, step, it):
        if it == S:
            return 38 if toward > 0 else 39
        return (0 if toward > 0 else 10) + ((step - 2) * 3 + it if step > 1 else 9)

    def begin(toward, step, it):
        far = step == 1
        target = ((right2 if far else right) if toward > 0 else (left2 if far else left))
        k = 4 if far else toward * (5 - step)
        push(r_index(toward, step, it), m_part(k, *item[it]), z_slot(toward, step, it), target)

    def extend(toward, step, it):
        here = z_slot(toward, step - 1, it)
        landed(r_index(toward, step - 1, it), here)
        value = here[...] + m_part(toward * (5 - step), *item[it])[...]
        if step == 3 and it == (A if toward > 0 else B):
            far = z_slot(toward, 1, it)
            landed(r_index(toward, 1, it), far)
            value += far[...]
        here[...] = value
        push(
            r_index(toward, step, it), here, z_slot(toward, step, it), right if toward > 0 else left
        )

    def merge(toward):
        here = z_slot(toward, 2, S)
        landed(r_index(toward, 2, S), here)
        m_part(2 * toward, 1, 1)[...] += here[...]

    def finish(it):
        value = m_part(0, *item[it])[...]
        for toward in (1, -1):
            here = z_slot(toward, 4, it)
            landed(r_index(toward, 4, it), here)
            value += here[...]
        return value

    counts = responsibilities(0, None)
    for i in range(2):
        moments(2, slice(i * width, (i + 1) * width), slice(0, rows // 2))
    counts = responsibilities(1, counts)
    counts = counts + pltpu.roll(counts, 64, 1)
    mbuf[:, 2 * width :] = counts
    for i in range(0, n_z * 2 * chunk, own):
        mbuf[i + part : i + own, 2 * width :] = jnp.where(
            low_lanes, counts[i : i + part], counts[i + part : i + own]
        )
    moments_half(2, 0)
    moments_half(2, 1)
    moments_half(1, 0)
    add_sibling(2)
    give(4, 0)
    give(4, 1)
    begin(1, 2, S)
    begin(-1, 2, S)
    begin(1, 2, Q)
    begin(-1, 2, Q)
    moments_half(1, 1)
    begin(1, 2, B)
    begin(-1, 2, A)
    begin(1, 2, A)
    begin(-1, 2, B)
    moments_half(0, 0)
    add_sibling(1)
    merge(1)
    give(2, 1)
    merge(-1)
    give(-2, 1)
    take(4, 0)
    begin(1, 1, A)
    take(4, 1)
    begin(-1, 1, B)
    extend(1, 3, Q)
    extend(-1, 3, Q)
    moments_half(0, 1)
    extend(-1, 3, A)
    add_sibling(0)
    give(1, 1)
    give(-1, 1)
    give(0, 1)
    take(2, 1)
    extend(1, 3, B)
    extend(1, 4, Q)
    extend(-1, 4, Q)
    extend(1, 3, A)
    take(-2, 1)
    extend(-1, 3, B)
    extend(-1, 4, A)
    take(1, 1)
    extend(1, 4, B)
    m_part(0, 1, 0)[...] = finish(Q)
    give(0, 0)
    extend(1, 4, A)
    take(-1, 1)
    extend(-1, 4, B)
    take(0, 1)
    sums_ref[part:, :] = finish(B)
    last = finish(A)
    here = xbuf.at[0, :, span(0)]
    landed(20, here)
    sums_ref[0:part, 0 : 2 * width] = last + here[...]

    for copy in sent:
        copy.wait_send()

    def stat_sent(t, carry):
        stat_copy(0, t).wait_send()
        stat_copy(1, t).wait_send()
        return carry

    lax.fori_loop(1, n_comp, stat_sent, 0)


def solution(mesh):
    n_dp, n_comp = mesh.shape["dp"], mesh.shape["comp"]
    n_z = n_dp // 4

    def per_device(embeddings, comp_means, comp_variances, comp_mass):
        rows, width = embeddings.shape
        own = comp_means.shape[0]
        group = own * n_dp
        wide = 2 * width + 128
        tiles = rows // 128
        f32, bf16 = jnp.float32, jnp.bfloat16
        vmem, dma = pltpu.VMEM, pltpu.SemaphoreType.DMA
        inside = pl.BlockSpec(memory_space=pltpu.VMEM)
        mass = comp_mass.reshape(1, own)
        sums = pl.pallas_call(
            functools.partial(kernel, n_z, n_comp),
            out_shape=jax.ShapeDtypeStruct((own, wide), f32),
            in_specs=[pl.BlockSpec(memory_space=pl.ANY), inside, inside, inside],
            out_specs=inside,
            scratch_shapes=[
                vmem((rows, width), f32),
                vmem((group, wide), f32),
                vmem((24 * own, 2 * width), bf16),
                vmem((group, 128), f32),
                vmem((rows, 2 * width), bf16),
                vmem((rows, 2 * width), bf16),
                vmem((group, rows), f32),
                vmem((2, n_comp, tiles // 2, 128), f32),
                vmem((tiles, 128), f32),
                vmem((2 * group, rows), bf16),
                vmem((group, wide), f32),
                vmem((group // 2, wide), f32),
                vmem((22, own // 2, wide), f32),
                vmem((10, own // 2, wide), f32),
                dma, dma((40,)), dma((40,)), dma((2, n_comp)), dma((2, n_comp)), dma((40,)), dma((40,)),
            ],
            compiler_params=pltpu.CompilerParams(
                collective_id=0, has_side_effects=True, vmem_limit_bytes=56 * 1024 * 1024
            ),
        )(embeddings, comp_means, comp_variances, mass)
        new_means, new_variances, new_mass = pl.pallas_call(
            functools.partial(update, (group * n_comp) / (rows * n_dp)),
            out_shape=[
                jax.ShapeDtypeStruct((own, width), f32),
                jax.ShapeDtypeStruct((own, width), f32),
                jax.ShapeDtypeStruct((1, own), f32),
            ],
            in_specs=[inside] * 4,
            out_specs=[inside] * 3,
        )(sums, comp_means, comp_variances, mass)
        return new_means, new_variances, new_mass.reshape(own)

    placed = (P("dp", None), P(("comp", "dp"), None), P(("comp", "dp"), None), P(("comp", "dp")))
    return jax.shard_map(
        per_device,
        mesh=mesh,
        in_specs=placed,
        out_specs=(P(("comp", "dp"), None), P(("comp", "dp"), None), P(("comp", "dp"))),
        check_vma=False,
    )
```

```python
import functools

import jax
import jax.numpy as jnp
from jax import lax
from jax.experimental import pallas as pl
from jax.experimental.pallas import tpu as pltpu
from jax.sharding import PartitionSpec as P

MESH = pl.DeviceIdType.MESH
NT = (((1,), (1,)), ((), ()))
NN = (((1,), (0,)), ((), ()))


def split(value):
    high = value.astype(jnp.bfloat16)
    return high, (value - high.astype(jnp.float32)).astype(jnp.bfloat16)


def diagonal(n):
    return lax.broadcasted_iota(jnp.int32, (n, n), 0) == lax.broadcasted_iota(jnp.int32, (n, n), 1)


def column(row):
    n = row.shape[1]
    return jnp.sum(jnp.where(diagonal(n), jnp.broadcast_to(row, (n, n)), 0.0), axis=1, keepdims=True)


def update(
    mass_scale, sums_ref, mean_ref, var_ref, mass_ref, new_mean_ref, new_var_ref, new_mass_ref
):
    own, width = mean_ref.shape
    mass = column(mass_ref[...])
    part = own // 2
    tile = sums_ref[part:, 2 * width :]
    low_lanes = lax.broadcasted_iota(jnp.int32, tile.shape, 1) < 64
    counts = jnp.concatenate(
        [
            jnp.sum(jnp.where(low_lanes, tile, 0.0), axis=1, keepdims=True),
            jnp.sum(jnp.where(low_lanes, 0.0, tile), axis=1, keepdims=True),
        ]
    )
    kept = 0.4 * mass
    new_mass = kept + 0.6 * mass_scale * counts
    means, variances = mean_ref[...], var_ref[...]
    first = kept * means + 0.6 * mass_scale * sums_ref[:, width : 2 * width]
    second = kept * (variances + means * means) + 0.6 * mass_scale * sums_ref[:, 0:width]
    new_means = first / new_mass
    new_mean_ref[...] = new_means
    new_var_ref[...] = second / new_mass - new_means * new_means
    new_mass_ref[...] = jnp.sum(
        jnp.where(diagonal(own), jnp.broadcast_to(new_mass, (own, own)), 0.0), axis=0, keepdims=True
    )


def kernel(
    n_z, n_comp,
    emb_hbm, mean_ref, var_ref, mass_ref,
    sums_ref,
    emb, wbuf, lhs, offs, xx_hi, xx_lo, st, stats, fac, rt,
    mbuf, sbuf, zbuf, xbuf,
    emb_sem, gs, gr, ss, sr, ms, mr,
):
    f32 = jnp.float32
    rows, width = emb.shape
    own = mean_ref.shape[0]
    part = own // 2
    chunk = 2 * own
    half = n_z * chunk
    tiles = rows // 128
    dp, comp = lax.axis_index("dp"), lax.axis_index("comp")
    z, xh, core = dp // 4, (dp // 2) % 2, dp % 2
    other_x, other_core = 1 - xh, 1 - core

    def at(zz, xx, cc):
        return (zz * 4 + xx * 2 + cc, comp)

    def z_off(k):
        return (z + k + n_z) % n_z

    right, left = at(z_off(1), xh, core), at(z_off(-1), xh, core)
    right2, left2 = at(z_off(2), xh, core), at(z_off(-2), xh, core)
    partner = (z * 4 + other_x * 2 + core, (comp + n_comp // 2) % n_comp)
    sibling = at(z, xh, other_core)

    emb_copy = pltpu.make_async_copy(emb_hbm, emb, emb_sem)
    emb_copy.start()
    barrier = pltpu.get_barrier_semaphore()
    for target in (right, left, right2, left2, partner, sibling):
        pl.semaphore_signal(barrier, inc=1, device_id=target, device_id_type=MESH)

    def greet(t, carry):
        peer = (dp, (comp + t) % n_comp)
        pl.semaphore_signal(barrier, inc=1, device_id=peer, device_id_type=MESH)
        return carry

    lax.fori_loop(1, n_comp, greet, 0)

    means, variances = mean_ref[...], var_ref[...]
    precision = 1.0 / variances
    mean_prec = means * precision
    mass = column(mass_ref[...])
    offset = jnp.log(mass) - 0.5 * jnp.sum(
        jnp.log(variances) + means * mean_prec, axis=1, keepdims=True
    )

    def w_rows(cc, zz, xx):
        return pl.ds(pl.multiple_of(cc * half + zz * chunk + xx * own, own), own)

    mine = w_rows(core, z, xh)
    wbuf[mine, 0:width] = -0.5 * precision
    wbuf[mine, width : 2 * width] = mean_prec
    low_lanes = lax.broadcasted_iota(jnp.int32, (part, 128), 1) < 64
    second = pl.ds(pl.multiple_of(core * half + z * chunk + xh * own + part, part), part)
    wbuf[second, 2 * width :] = jnp.where(
        low_lanes,
        jnp.broadcast_to(offset[0:part], (part, 128)),
        jnp.broadcast_to(offset[part:own], (part, 128)),
    )

    pl.semaphore_wait(barrier, 6 + n_comp - 1)

    cols = (xh, other_x)
    sent = []

    def gather_copy(index, k, c, p, target, n=part):
        start = core * half + z_off(k) * chunk + (cols[c] * own if n < chunk else 0) + p * part
        place = pl.ds(pl.multiple_of(start, part), n)
        span = slice(0, 2 * width) if n == part and p == 0 else slice(0, 2 * width + 128)
        return pltpu.make_async_remote_copy(
            src_ref=wbuf.at[place, span], dst_ref=wbuf.at[place, span],
            send_sem=gs.at[index], recv_sem=gr.at[index],
            device_id=target, device_id_type=MESH,
        )

    def send(index, k, c, p, target, n=part):
        copy = gather_copy(index, k, c, p, target, n)
        copy.start()
        sent.append(copy)

    def arrived(index, p, n=part):
        gather_copy(index, 0, 0, p, partner, n).wait_recv()

    A, B, Q, S = 0, 1, 2, 3
    item = {A: (0, 0), B: (0, 1), Q: (1, 0), S: (1, 1)}

    def ring(toward, step, it):
        if it == S:
            return 38 if toward > 0 else 39
        return (0 if toward > 0 else 10) + ((step - 1) * 3 + it if step < 4 else 9)

    def around(toward, step, it):
        far = step == 4
        target = ((right2 if far else right) if toward > 0 else (left2 if far else left))
        send(ring(toward, step, it), -toward * (2 if far else step - 1), *item[it], target)

    def came(toward, step, it):
        arrived(ring(toward, step, it), item[it][1])

    def x_index(k, p):
        return 20 + {(0, 0): 0, (0, 1): 1, (4, 0): 8, (4, 1): 9}.get((k, p), 1 + 2 * abs(k) - (k < 0))

    def across(k, p):
        send(x_index(k, p), k, 0, p, partner)

    def crossed(k, p):
        arrived(x_index(k, p), p)

    def to_sibling(k):
        send(30 + k % 8, k, 0, 0, sibling, chunk)

    around(1, 1, A)
    around(-1, 1, B)
    across(0, 0)
    around(1, 1, B)
    around(-1, 1, A)
    across(0, 1)

    emb_copy.wait()

    def prepare(i, carry):
        place = pl.ds(pl.multiple_of(i * 128, 128), 128)
        x = emb[place, :]
        hi, lo = split(x * x)
        xx_hi[place, 0:width] = hi
        xx_lo[place, 0:width] = lo
        hi, lo = split(x)
        xx_hi[place, width:] = hi
        xx_lo[place, width:] = lo
        return carry

    lax.fori_loop(0, tiles // 2, prepare, 0)
    lax.fori_loop(tiles // 2, tiles, prepare, 0)

    groups = ((0, -1, 1), (-2, 2), (-3, 3, 4))
    bases = [2 * chunk * sum(len(g) for g in groups[:i]) for i in range(3)]

    def stage(g):
        n, base = 2 * chunk * len(groups[g]), bases[g]
        places = [(cc, z_off(k)) for cc in (core, other_core) for k in groups[g]]
        for i, (cc, zz) in enumerate(places):
            place = pl.ds(pl.multiple_of(cc * half + zz * chunk, chunk), chunk)
            hi, lo = split(wbuf[place, 0 : 2 * width])
            lhs[i * chunk : (i + 1) * chunk, :] = hi
            lhs[n + i * chunk : n + (i + 1) * chunk, :] = lo
            tile = wbuf[place, 2 * width :]
            for r in range(0, chunk, part):
                both = tile[r // own * own + part : r // own * own + own]
                lane = 64 * (r % own // part)
                offs[base + i * chunk + r : base + i * chunk + r + part, :] = jnp.broadcast_to(
                    both[:, lane : lane + 1], (part, 128)
                )

    def score(g, first, last, block):
        n, base = 2 * chunk * len(groups[g]), bases[g]
        for b in range(first, last, block):
            place = slice(b, b + block)
            both = lax.dot_general(
                lhs[0 : 2 * n, :], xx_hi[place, :], NT, preferred_element_type=f32
            )
            low = lax.dot_general(lhs[0:n, :], xx_lo[place, :], NT, preferred_element_type=f32)
            off = jnp.concatenate([offs[base : base + n, :]] * (block // 128), 1)
            st[base : base + n, place] = both[:n] + both[n:] + low + off

    def sibling_arrived(g):
        for k in groups[g]:
            arrived(30 + k % 8, 0, chunk)

    came(1, 1, A)
    around(1, 2, A)
    came(-1, 1, B)
    around(-1, 2, B)
    across(1, 1)
    crossed(0, 0)
    around(1, 1, Q)
    around(-1, 1, Q)
    came(1, 1, B)
    around(1, 2, B)
    across(-1, 1)
    came(-1, 1, A)
    around(-1, 2, A)
    crossed(0, 1)
    to_sibling(0)
    came(1, 2, A)
    around(1, 4, A)
    came(-1, 2, B)
    around(-1, 4, B)
    across(2, 1)
    came(1, 1, Q)
    around(1, 2, Q)
    came(-1, 1, Q)
    around(-1, 2, Q)
    crossed(1, 1)
    to_sibling(1)
    came(1, 2, B)
    across(-2, 1)
    came(-1, 2, A)
    around(1, 3, A)
    around(-1, 3, B)
    around(1, 3, B)
    around(-1, 3, A)
    crossed(-1, 1)
    to_sibling(-1)
    sibling_arrived(0)
    stage(0)
    score(0, 0, rows // 2, rows // 2)
    came(1, 2, Q)
    around(1, 3, Q)
    came(-1, 2, Q)
    around(-1, 3, Q)
    came(-1, 3, B)
    crossed(2, 1)
    around(-1, 3, S)
    to_sibling(2)
    came(1, 4, A)
    across(4, 0)
    came(-1, 4, B)
    across(4, 1)
    came(1, 3, B)
    crossed(-2, 1)
    around(1, 3, S)
    to_sibling(-2)
    score(0, rows // 2, rows, rows // 2)
    sibling_arrived(1)
    stage(1)
    score(1, 0, rows // 2, rows // 2)
    came(1, 3, A)
    came(-1, 3, A)
    came(1, 3, Q)
    came(-1, 3, Q)
    came(-1, 3, S)
    to_sibling(3)
    came(1, 3, S)
    to_sibling(-3)
    score(1, rows // 2, rows, rows // 2)
    crossed(4, 0)
    crossed(4, 1)
    to_sibling(4)
    sibling_arrived(2)
    stage(2)

    def statistic(h):
        for j in range(tiles // 2):
            i = h * tiles // 2 + j
            lanes = slice(i * 128, (i + 1) * 128)
            s = st[:, lanes]
            peak = jnp.max(s, axis=0, keepdims=True)
            e = jnp.exp(s - peak)
            st[:, lanes] = e
            fac[i : i + 1, :] = peak
            stats[h, comp, j : j + 1, :] = peak + jnp.log(jnp.sum(e, axis=0, keepdims=True))

    def stat_copy(h, t):
        return pltpu.make_async_remote_copy(
            src_ref=stats.at[h, comp], dst_ref=stats.at[h, comp],
            send_sem=ss.at[h, t], recv_sem=sr.at[h, t],
            device_id=(dp, (comp + t) % n_comp), device_id_type=MESH,
        )

    def stat_start(h):
        for t in range(1, n_comp):
            stat_copy(h, t).start()

    def factors(h):
        for t in range(1, n_comp):
            stat_copy(h, t).wait_recv()
        logs = stats[h]
        peak = jnp.max(logs, axis=0)
        total = jnp.sum(jnp.exp(logs - peak[None]), axis=0)
        mine = slice(h * tiles // 2, (h + 1) * tiles // 2)
        fac[mine, :] = jnp.exp(fac[mine, :] - peak) / total

    def responsibilities(h, g):
        n, base = 2 * chunk * len(groups[g]), bases[g]
        counts = mbuf[base : base + n, 2 * width :] if h else None
        for i in range(h * tiles // 2, (h + 1) * tiles // 2):
            lanes = slice(i * 128, (i + 1) * 128)
            resp = st[base : base + n, lanes] * fac[i : i + 1, :]
            counts = resp if counts is None else counts + resp
            hi, lo = split(resp)
            rt[2 * base : 2 * base + n, lanes] = hi
            rt[2 * base + n : 2 * base + 2 * n, lanes] = lo
        mbuf[base : base + n, 2 * width :] = counts

    def fold_counts(g):
        n, base = 2 * chunk * len(groups[g]), bases[g]
        counts = mbuf[base : base + n, 2 * width :]
        counts = counts + pltpu.roll(counts, 64, 1)
        for i in range(0, n, own):
            mbuf[base + i + part : base + i + own, 2 * width :] = jnp.where(
                low_lanes, counts[i : i + part], counts[i + part : i + own]
            )

    score(2, 0, rows // 2, rows // 2)
    statistic(0)
    stat_start(0)
    score(2, rows // 2, rows, rows // 2)
    statistic(1)
    stat_start(1)

    def moments(g, lanes, over=slice(None), add=False):
        n, base = 2 * chunk * len(groups[g]), bases[g]
        both = lax.dot_general(
            rt[2 * base : 2 * base + 2 * n, over], xx_hi[over, lanes], NN, preferred_element_type=f32
        )
        low = lax.dot_general(
            rt[2 * base : 2 * base + n, over], xx_lo[over, lanes], NN, preferred_element_type=f32
        )
        value = both[:n] + both[n:] + low
        mbuf[base : base + n, lanes] = mbuf[base : base + n, lanes] + value if add else value

    def reduce_copy(index, src, dst, target):
        return pltpu.make_async_remote_copy(
            src_ref=src, dst_ref=dst, send_sem=ms.at[index], recv_sem=mr.at[index],
            device_id=target, device_id_type=MESH,
        )

    def push(index, src, dst, target):
        copy = reduce_copy(index, src, dst, target)
        copy.start()
        sent.append(copy)

    def landed(index, dst):
        reduce_copy(index, dst, dst, partner).wait_recv()

    lanes_of = (slice(0, width), slice(width, 2 * width + 128))

    def spot(g, i):
        h, base = chunk * len(groups[g]), bases[g]
        return sbuf.at[base // 2 : base // 2 + h, lanes_of[i]]

    def moments_half(g, i):
        h, base = chunk * len(groups[g]), bases[g]
        lanes = slice(i * width, (i + 1) * width)
        if g == 2:
            moments(g, lanes, slice(rows // 2, rows), True)
        else:
            moments(g, lanes)
        push(30 + 2 * g + i, mbuf.at[base + h : base + 2 * h, lanes_of[i]], spot(g, i), sibling)

    def add_sibling(g):
        h, base = chunk * len(groups[g]), bases[g]
        for i in range(2):
            landed(30 + 2 * g + i, spot(g, i))
            mbuf[base : base + h, lanes_of[i]] += spot(g, i)[...]

    def span(p):
        return slice(0, 2 * width + (128 if p else 0))

    def z_slot(toward, step, it):
        i = r_index(toward, step, it)
        return zbuf.at[i if it < S else i - 18, :, span(item[it][1])]

    def m_rows(k, c, p):
        g = [i for i in range(3) if k in groups[i]][0]
        start = bases[g] + groups[g].index(k) * chunk + cols[c] * own + p * part
        return pl.ds(pl.multiple_of(start, part), part)

    def m_part(k, c, p):
        return mbuf.at[m_rows(k, c, p), span(p)]

    def give(k, p):
        i = x_index(k, p)
        push(i, m_part(k, 1, p), xbuf.at[i - 20, :, span(p)], partner)

    def take(k, p):
        i = x_index(k, p)
        here = xbuf.at[i - 20, :, span(p)]
        landed(i, here)
        m_part(k, 0, p)[...] += here[...]

    def r_index(toward, step, it):
        if it == S:
            return 38 if toward > 0 else 39
        return (0 if toward > 0 else 10) + ((step - 2) * 3 + it if step > 1 else 9)

    def begin(toward, step, it):
        far = step == 1
        target = ((right2 if far else right) if toward > 0 else (left2 if far else left))
        k = 4 if far else toward * (5 - step)
        push(r_index(toward, step, it), m_part(k, *item[it]), z_slot(toward, step, it), target)

    def extend(toward, step, it):
        here = z_slot(toward, step - 1, it)
        landed(r_index(toward, step - 1, it), here)
        value = here[...] + m_part(toward * (5 - step), *item[it])[...]
        if step == 3 and it == (A if toward > 0 else B):
            far = z_slot(toward, 1, it)
            landed(r_index(toward, 1, it), far)
            value += far[...]
        here[...] = value
        push(
            r_index(toward, step, it), here, z_slot(toward, step, it), right if toward > 0 else left
        )

    def merge(toward):
        here = z_slot(toward, 2, S)
        landed(r_index(toward, 2, S), here)
        m_part(2 * toward, 1, 1)[...] += here[...]

    def finish(it):
        value = m_part(0, *item[it])[...]
        for toward in (1, -1):
            here = z_slot(toward, 4, it)
            landed(r_index(toward, 4, it), here)
            value += here[...]
        return value

    factors(0)
    responsibilities(0, 2)
    for i in range(2):
        moments(2, slice(i * width, (i + 1) * width), slice(0, rows // 2))
    responsibilities(0, 1)
    responsibilities(0, 0)
    factors(1)
    responsibilities(1, 2)
    moments_half(2, 0)
    fold_counts(2)
    moments_half(2, 1)
    responsibilities(1, 1)
    fold_counts(1)
    moments_half(1, 0)
    add_sibling(2)
    give(4, 0)
    give(4, 1)
    begin(1, 2, S)
    begin(-1, 2, S)
    begin(1, 2, Q)
    begin(-1, 2, Q)
    moments_half(1, 1)
    begin(1, 2, B)
    begin(-1, 2, A)
    begin(1, 2, A)
    begin(-1, 2, B)
    responsibilities(1, 0)
    fold_counts(0)
    moments_half(0, 0)
    add_sibling(1)
    merge(1)
    give(2, 1)
    merge(-1)
    give(-2, 1)
    take(4, 0)
    begin(1, 1, A)
    take(4, 1)
    begin(-1, 1, B)
    extend(1, 3, Q)
    extend(-1, 3, Q)
    moments_half(0, 1)
    extend(-1, 3, A)
    add_sibling(0)
    give(1, 1)
    give(-1, 1)
    give(0, 1)
    take(2, 1)
    extend(1, 3, B)
    extend(1, 4, Q)
    extend(-1, 4, Q)
    extend(1, 3, A)
    take(-2, 1)
    extend(-1, 3, B)
    extend(-1, 4, A)
    take(1, 1)
    extend(1, 4, B)
    m_part(0, 1, 0)[...] = finish(Q)
    give(0, 0)
    extend(1, 4, A)
    take(-1, 1)
    extend(-1, 4, B)
    take(0, 1)
    sums_ref[part:, :] = finish(B)
    last = finish(A)
    here = xbuf.at[0, :, span(0)]
    landed(20, here)
    sums_ref[0:part, 0 : 2 * width] = last + here[...]

    for copy in sent:
        copy.wait_send()

    def stat_sent(t, carry):
        stat_copy(0, t).wait_send()
        stat_copy(1, t).wait_send()
        return carry

    lax.fori_loop(1, n_comp, stat_sent, 0)


def solution(mesh):
    n_dp, n_comp = mesh.shape["dp"], mesh.shape["comp"]
    n_z = n_dp // 4

    def per_device(embeddings, comp_means, comp_variances, comp_mass):
        rows, width = embeddings.shape
        own = comp_means.shape[0]
        group = own * n_dp
        wide = 2 * width + 128
        tiles = rows // 128
        f32, bf16 = jnp.float32, jnp.bfloat16
        vmem, dma = pltpu.VMEM, pltpu.SemaphoreType.DMA
        inside = pl.BlockSpec(memory_space=pltpu.VMEM)
        mass = comp_mass.reshape(1, own)
        sums = pl.pallas_call(
            functools.partial(kernel, n_z, n_comp),
            out_shape=jax.ShapeDtypeStruct((own, wide), f32),
            in_specs=[pl.BlockSpec(memory_space=pl.ANY), inside, inside, inside],
            out_specs=inside,
            scratch_shapes=[
                vmem((rows, width), f32),
                vmem((group, wide), f32),
                vmem((24 * own, 2 * width), bf16),
                vmem((group, 128), f32),
                vmem((rows, 2 * width), bf16),
                vmem((rows, 2 * width), bf16),
                vmem((group, rows), f32),
                vmem((2, n_comp, tiles // 2, 128), f32),
                vmem((tiles, 128), f32),
                vmem((2 * group, rows), bf16),
                vmem((group, wide), f32),
                vmem((group // 2, wide), f32),
                vmem((22, own // 2, wide), f32),
                vmem((10, own // 2, wide), f32),
                dma, dma((40,)), dma((40,)), dma((2, n_comp)), dma((2, n_comp)), dma((40,)), dma((40,)),
            ],
            compiler_params=pltpu.CompilerParams(
                collective_id=0, has_side_effects=True, vmem_limit_bytes=56 * 1024 * 1024
            ),
        )(embeddings, comp_means, comp_variances, mass)
        new_means, new_variances, new_mass = pl.pallas_call(
            functools.partial(update, (group * n_comp) / (rows * n_dp)),
            out_shape=[
                jax.ShapeDtypeStruct((own, width), f32),
                jax.ShapeDtypeStruct((own, width), f32),
                jax.ShapeDtypeStruct((1, own), f32),
            ],
            in_specs=[inside] * 4,
            out_specs=[inside] * 3,
        )(sums, comp_means, comp_variances, mass)
        return new_means, new_variances, new_mass.reshape(own)

    placed = (P("dp", None), P(("comp", "dp"), None), P(("comp", "dp"), None), P(("comp", "dp")))
    return jax.shard_map(
        per_device,
        mesh=mesh,
        in_specs=placed,
        out_specs=(P(("comp", "dp"), None), P(("comp", "dp"), None), P(("comp", "dp"))),
        check_vma=False,
    )
```

```python
import functools

import jax
import jax.numpy as jnp
from jax import lax
from jax.experimental import pallas as pl
from jax.experimental.pallas import tpu as pltpu
from jax.sharding import PartitionSpec as P

MESH = pl.DeviceIdType.MESH
NT = (((1,), (1,)), ((), ()))
NN = (((1,), (0,)), ((), ()))


def split(value):
    high = value.astype(jnp.bfloat16)
    return high, (value - high.astype(jnp.float32)).astype(jnp.bfloat16)


def diagonal(n):
    return lax.broadcasted_iota(jnp.int32, (n, n), 0) == lax.broadcasted_iota(jnp.int32, (n, n), 1)


def column(row):
    n = row.shape[1]
    return jnp.sum(jnp.where(diagonal(n), jnp.broadcast_to(row, (n, n)), 0.0), axis=1, keepdims=True)


def update(
    mass_scale, sums_ref, mean_ref, var_ref, mass_ref, new_mean_ref, new_var_ref, new_mass_ref
):
    own, width = mean_ref.shape
    mass = column(mass_ref[...])
    part = own // 2
    tile = sums_ref[part:, 2 * width :]
    low_lanes = lax.broadcasted_iota(jnp.int32, tile.shape, 1) < 64
    counts = jnp.concatenate(
        [
            jnp.sum(jnp.where(low_lanes, tile, 0.0), axis=1, keepdims=True),
            jnp.sum(jnp.where(low_lanes, 0.0, tile), axis=1, keepdims=True),
        ]
    )
    kept = 0.4 * mass
    new_mass = kept + 0.6 * mass_scale * counts
    means, variances = mean_ref[...], var_ref[...]
    first = kept * means + 0.6 * mass_scale * sums_ref[:, width : 2 * width]
    second = kept * (variances + means * means) + 0.6 * mass_scale * sums_ref[:, 0:width]
    new_means = first / new_mass
    new_mean_ref[...] = new_means
    new_var_ref[...] = second / new_mass - new_means * new_means
    new_mass_ref[...] = jnp.sum(
        jnp.where(diagonal(own), jnp.broadcast_to(new_mass, (own, own)), 0.0), axis=0, keepdims=True
    )


def kernel(
    n_z, n_comp,
    emb_hbm, mean_ref, var_ref, mass_ref,
    sums_ref,
    emb, wbuf, lhs, offs, xx_hi, xx_lo, st, stats, fac, rt,
    mbuf, sbuf, zbuf, xbuf,
    emb_sem, gs, gr, ss, sr, ms, mr,
):
    f32 = jnp.float32
    rows, width = emb.shape
    own = mean_ref.shape[0]
    part = own // 2
    chunk = 2 * own
    half = n_z * chunk
    tiles = rows // 128
    dp, comp = lax.axis_index("dp"), lax.axis_index("comp")
    z, xh, core = dp // 4, (dp // 2) % 2, dp % 2
    other_x, other_core = 1 - xh, 1 - core

    def at(zz, xx, cc):
        return (zz * 4 + xx * 2 + cc, comp)

    def z_off(k):
        return (z + k + n_z) % n_z

    right, left = at(z_off(1), xh, core), at(z_off(-1), xh, core)
    right2, left2 = at(z_off(2), xh, core), at(z_off(-2), xh, core)
    partner = (z * 4 + other_x * 2 + core, (comp + n_comp // 2) % n_comp)
    sibling = at(z, xh, other_core)

    emb_copy = pltpu.make_async_copy(emb_hbm, emb, emb_sem)
    emb_copy.start()
    barrier = pltpu.get_barrier_semaphore()
    for target in (right, left, right2, left2, partner, sibling):
        pl.semaphore_signal(barrier, inc=1, device_id=target, device_id_type=MESH)

    def greet(t, carry):
        peer = (dp, (comp + t) % n_comp)
        pl.semaphore_signal(barrier, inc=1, device_id=peer, device_id_type=MESH)
        return carry

    lax.fori_loop(1, n_comp, greet, 0)

    means, variances = mean_ref[...], var_ref[...]
    precision = 1.0 / variances
    mean_prec = means * precision
    mass = column(mass_ref[...])
    offset = jnp.log(mass) - 0.5 * jnp.sum(
        jnp.log(variances) + means * mean_prec, axis=1, keepdims=True
    )

    def w_rows(cc, zz, xx):
        return pl.ds(pl.multiple_of(cc * half + zz * chunk + xx * own, own), own)

    mine = w_rows(core, z, xh)
    wbuf[mine, 0:width] = -0.5 * precision
    wbuf[mine, width : 2 * width] = mean_prec
    low_lanes = lax.broadcasted_iota(jnp.int32, (part, 128), 1) < 64
    second = pl.ds(pl.multiple_of(core * half + z * chunk + xh * own + part, part), part)
    wbuf[second, 2 * width :] = jnp.where(
        low_lanes,
        jnp.broadcast_to(offset[0:part], (part, 128)),
        jnp.broadcast_to(offset[part:own], (part, 128)),
    )

    pl.semaphore_wait(barrier, 6 + n_comp - 1)

    cols = (xh, other_x)
    sent = []

    def gather_copy(index, k, c, p, target, n=part):
        start = core * half + z_off(k) * chunk + (cols[c] * own if n < chunk else 0) + p * part
        place = pl.ds(pl.multiple_of(start, part), n)
        span = slice(0, 2 * width) if n == part and p == 0 else slice(0, 2 * width + 128)
        return pltpu.make_async_remote_copy(
            src_ref=wbuf.at[place, span], dst_ref=wbuf.at[place, span],
            send_sem=gs.at[index], recv_sem=gr.at[index],
            device_id=target, device_id_type=MESH,
        )

    def send(index, k, c, p, target, n=part):
        copy = gather_copy(index, k, c, p, target, n)
        copy.start()
        sent.append(copy)

    def arrived(index, p, n=part):
        gather_copy(index, 0, 0, p, partner, n).wait_recv()

    A, B, Q, S = 0, 1, 2, 3
    item = {A: (0, 0), B: (0, 1), Q: (1, 0), S: (1, 1)}

    def ring(toward, step, it):
        if it == S:
            return 38 if toward > 0 else 39
        return (0 if toward > 0 else 10) + ((step - 1) * 3 + it if step < 4 else 9)

    def around(toward, step, it):
        far = step == 4
        target = ((right2 if far else right) if toward > 0 else (left2 if far else left))
        send(ring(toward, step, it), -toward * (2 if far else step - 1), *item[it], target)

    def came(toward, step, it):
        arrived(ring(toward, step, it), item[it][1])

    def x_index(k, p):
        return 20 + {(0, 0): 0, (0, 1): 1, (4, 0): 8, (4, 1): 9}.get((k, p), 1 + 2 * abs(k) - (k < 0))

    def across(k, p):
        send(x_index(k, p), k, 0, p, partner)

    def crossed(k, p):
        arrived(x_index(k, p), p)

    def to_sibling(k):
        send(30 + k % 8, k, 0, 0, sibling, chunk)

    around(1, 1, A)
    around(-1, 1, B)
    across(0, 0)
    around(1, 1, B)
    around(-1, 1, A)
    across(0, 1)

    emb_copy.wait()

    def prepare(i, carry):
        place = pl.ds(pl.multiple_of(i * 128, 128), 128)
        x = emb[place, :]
        hi, lo = split(x * x)
        xx_hi[place, 0:width] = hi
        xx_lo[place, 0:width] = lo
        hi, lo = split(x)
        xx_hi[place, width:] = hi
        xx_lo[place, width:] = lo
        return carry

    lax.fori_loop(0, tiles // 2, prepare, 0)
    lax.fori_loop(tiles // 2, tiles, prepare, 0)

    groups = ((0, -1, 1), (-2, 2), (-3, 3, 4))
    bases = [2 * chunk * sum(len(g) for g in groups[:i]) for i in range(3)]

    def stage(g):
        n, base = 2 * chunk * len(groups[g]), bases[g]
        places = [(cc, z_off(k)) for cc in (core, other_core) for k in groups[g]]
        for i, (cc, zz) in enumerate(places):
            place = pl.ds(pl.multiple_of(cc * half + zz * chunk, chunk), chunk)
            hi, lo = split(wbuf[place, 0 : 2 * width])
            lhs[i * chunk : (i + 1) * chunk, :] = hi
            lhs[n + i * chunk : n + (i + 1) * chunk, :] = lo
            tile = wbuf[place, 2 * width :]
            for r in range(0, chunk, part):
                both = tile[r // own * own + part : r // own * own + own]
                lane = 64 * (r % own // part)
                offs[base + i * chunk + r : base + i * chunk + r + part, :] = jnp.broadcast_to(
                    both[:, lane : lane + 1], (part, 128)
                )

    def score(g, first, last, block):
        n, base = 2 * chunk * len(groups[g]), bases[g]
        for b in range(first, last, block):
            place = slice(b, b + block)
            both = lax.dot_general(
                lhs[0 : 2 * n, :], xx_hi[place, :], NT, preferred_element_type=f32
            )
            low = lax.dot_general(lhs[0:n, :], xx_lo[place, :], NT, preferred_element_type=f32)
            off = jnp.concatenate([offs[base : base + n, :]] * (block // 128), 1)
            st[base : base + n, place] = both[:n] + both[n:] + low + off

    def sibling_arrived(g):
        for k in groups[g]:
            arrived(30 + k % 8, 0, chunk)

    came(1, 1, A)
    around(1, 2, A)
    came(-1, 1, B)
    around(-1, 2, B)
    across(1, 1)
    crossed(0, 0)
    around(1, 1, Q)
    around(-1, 1, Q)
    came(1, 1, B)
    around(1, 2, B)
    across(-1, 1)
    came(-1, 1, A)
    around(-1, 2, A)
    crossed(0, 1)
    to_sibling(0)
    came(1, 2, A)
    around(1, 4, A)
    came(-1, 2, B)
    around(-1, 4, B)
    across(2, 1)
    came(1, 1, Q)
    around(1, 2, Q)
    came(-1, 1, Q)
    around(-1, 2, Q)
    crossed(1, 1)
    to_sibling(1)
    came(1, 2, B)
    across(-2, 1)
    came(-1, 2, A)
    around(1, 3, A)
    around(-1, 3, B)
    around(1, 3, B)
    around(-1, 3, A)
    crossed(-1, 1)
    to_sibling(-1)
    sibling_arrived(0)
    stage(0)
    score(0, 0, rows // 2, rows // 2)
    came(1, 2, Q)
    around(1, 3, Q)
    came(-1, 2, Q)
    around(-1, 3, Q)
    came(-1, 3, B)
    crossed(2, 1)
    around(-1, 3, S)
    to_sibling(2)
    came(1, 4, A)
    across(4, 0)
    came(-1, 4, B)
    across(4, 1)
    came(1, 3, B)
    crossed(-2, 1)
    around(1, 3, S)
    to_sibling(-2)
    score(0, rows // 2, rows, rows // 2)
    sibling_arrived(1)
    stage(1)
    score(1, 0, rows // 2, rows // 2)
    came(1, 3, A)
    came(-1, 3, A)
    came(1, 3, Q)
    came(-1, 3, Q)
    came(-1, 3, S)
    to_sibling(3)
    came(1, 3, S)
    to_sibling(-3)
    score(1, rows // 2, rows, rows // 2)
    crossed(4, 0)
    crossed(4, 1)
    to_sibling(4)
    sibling_arrived(2)
    stage(2)

    def statistic(h):
        for j in range(tiles // 2):
            i = h * tiles // 2 + j
            lanes = slice(i * 128, (i + 1) * 128)
            s = st[:, lanes]
            peak = jnp.max(s, axis=0, keepdims=True)
            e = jnp.exp(s - peak)
            st[:, lanes] = e
            fac[i : i + 1, :] = peak
            stats[h, comp, j : j + 1, :] = peak + jnp.log(jnp.sum(e, axis=0, keepdims=True))

    def stat_copy(h, t):
        return pltpu.make_async_remote_copy(
            src_ref=stats.at[h, comp], dst_ref=stats.at[h, comp],
            send_sem=ss.at[h, t], recv_sem=sr.at[h, t],
            device_id=(dp, (comp + t) % n_comp), device_id_type=MESH,
        )

    def stat_start(h):
        for t in range(1, n_comp):
            stat_copy(h, t).start()

    def factors(h):
        for t in range(1, n_comp):
            stat_copy(h, t).wait_recv()
        logs = stats[h]
        peak = jnp.max(logs, axis=0)
        total = jnp.sum(jnp.exp(logs - peak[None]), axis=0)
        mine = slice(h * tiles // 2, (h + 1) * tiles // 2)
        fac[mine, :] = jnp.exp(fac[mine, :] - peak) / total

    def responsibilities(h, g):
        n, base = 2 * chunk * len(groups[g]), bases[g]
        counts = mbuf[base : base + n, 2 * width :] if h else None
        for i in range(h * tiles // 2, (h + 1) * tiles // 2):
            lanes = slice(i * 128, (i + 1) * 128)
            resp = st[base : base + n, lanes] * fac[i : i + 1, :]
            counts = resp if counts is None else counts + resp
            hi, lo = split(resp)
            rt[2 * base : 2 * base + n, lanes] = hi
            rt[2 * base + n : 2 * base + 2 * n, lanes] = lo
        mbuf[base : base + n, 2 * width :] = counts

    def fold_counts(g):
        n, base = 2 * chunk * len(groups[g]), bases[g]
        counts = mbuf[base : base + n, 2 * width :]
        counts = counts + pltpu.roll(counts, 64, 1)
        for i in range(0, n, own):
            mbuf[base + i + part : base + i + own, 2 * width :] = jnp.where(
                low_lanes, counts[i : i + part], counts[i + part : i + own]
            )

    score(2, 0, rows // 2, rows // 2)
    statistic(0)
    stat_start(0)
    score(2, rows // 2, rows, rows // 2)
    statistic(1)
    stat_start(1)

    def moments(g, lanes, over=slice(None), add=False):
        n, base = 2 * chunk * len(groups[g]), bases[g]
        both = lax.dot_general(
            rt[2 * base : 2 * base + 2 * n, over], xx_hi[over, lanes], NN, preferred_element_type=f32
        )
        low = lax.dot_general(
            rt[2 * base : 2 * base + n, over], xx_lo[over, lanes], NN, preferred_element_type=f32
        )
        value = both[:n] + both[n:] + low
        mbuf[base : base + n, lanes] = mbuf[base : base + n, lanes] + value if add else value

    def reduce_copy(index, src, dst, target):
        return pltpu.make_async_remote_copy(
            src_ref=src, dst_ref=dst, send_sem=ms.at[index], recv_sem=mr.at[index],
            device_id=target, device_id_type=MESH,
        )

    def push(index, src, dst, target):
        copy = reduce_copy(index, src, dst, target)
        copy.start()
        sent.append(copy)

    def landed(index, dst):
        reduce_copy(index, dst, dst, partner).wait_recv()

    lanes_of = (slice(0, width), slice(width, 2 * width + 128))

    def spot(g, i):
        h, base = chunk * len(groups[g]), bases[g]
        return sbuf.at[base // 2 : base // 2 + h, lanes_of[i]]

    def moments_half(g, i):
        h, base = chunk * len(groups[g]), bases[g]
        lanes = slice(i * width, (i + 1) * width)
        if g == 2:
            moments(g, lanes, slice(rows // 2, rows), True)
        else:
            moments(g, lanes)
        push(30 + 2 * g + i, mbuf.at[base + h : base + 2 * h, lanes_of[i]], spot(g, i), sibling)

    def add_sibling(g):
        h, base = chunk * len(groups[g]), bases[g]
        for i in range(2):
            landed(30 + 2 * g + i, spot(g, i))
            mbuf[base : base + h, lanes_of[i]] += spot(g, i)[...]

    def span(p):
        return slice(0, 2 * width + (128 if p else 0))

    def z_slot(toward, step, it):
        i = r_index(toward, step, it)
        return zbuf.at[i if it < S else i - 18, :, span(item[it][1])]

    def m_rows(k, c, p):
        g = [i for i in range(3) if k in groups[i]][0]
        start = bases[g] + groups[g].index(k) * chunk + cols[c] * own + p * part
        return pl.ds(pl.multiple_of(start, part), part)

    def m_part(k, c, p):
        return mbuf.at[m_rows(k, c, p), span(p)]

    def give(k, p):
        i = x_index(k, p)
        push(i, m_part(k, 1, p), xbuf.at[i - 20, :, span(p)], partner)

    def take(k, p):
        i = x_index(k, p)
        here = xbuf.at[i - 20, :, span(p)]
        landed(i, here)
        m_part(k, 0, p)[...] += here[...]

    def r_index(toward, step, it):
        if it == S:
            return 38 if toward > 0 else 39
        return (0 if toward > 0 else 10) + ((step - 2) * 3 + it if step > 1 else 9)

    def begin(toward, step, it):
        far = step == 1
        target = ((right2 if far else right) if toward > 0 else (left2 if far else left))
        k = 4 if far else toward * (5 - step)
        push(r_index(toward, step, it), m_part(k, *item[it]), z_slot(toward, step, it), target)

    def extend(toward, step, it):
        here = z_slot(toward, step - 1, it)
        landed(r_index(toward, step - 1, it), here)
        value = here[...] + m_part(toward * (5 - step), *item[it])[...]
        if step == 3 and it == (A if toward > 0 else B):
            far = z_slot(toward, 1, it)
            landed(r_index(toward, 1, it), far)
            value += far[...]
        here[...] = value
        push(
            r_index(toward, step, it), here, z_slot(toward, step, it), right if toward > 0 else left
        )

    def merge(toward):
        here = z_slot(toward, 2, S)
        landed(r_index(toward, 2, S), here)
        m_part(2 * toward, 1, 1)[...] += here[...]

    def finish(it):
        value = m_part(0, *item[it])[...]
        for toward in (1, -1):
            here = z_slot(toward, 4, it)
            landed(r_index(toward, 4, it), here)
            value += here[...]
        return value

    factors(0)
    responsibilities(0, 2)
    for i in range(2):
        moments(2, slice(i * width, (i + 1) * width), slice(0, rows // 2))
    responsibilities(0, 1)
    responsibilities(0, 0)
    factors(1)
    responsibilities(1, 2)
    moments_half(2, 0)
    fold_counts(2)
    moments_half(2, 1)
    responsibilities(1, 1)
    fold_counts(1)
    add_sibling(2)
    give(4, 0)
    give(4, 1)
    begin(1, 2, S)
    begin(-1, 2, S)
    begin(1, 2, Q)
    begin(-1, 2, Q)
    moments_half(1, 0)
    moments_half(1, 1)
    begin(1, 2, B)
    begin(-1, 2, A)
    begin(1, 2, A)
    begin(-1, 2, B)
    responsibilities(1, 0)
    fold_counts(0)
    moments_half(0, 0)
    add_sibling(1)
    merge(1)
    give(2, 1)
    merge(-1)
    give(-2, 1)
    extend(1, 3, Q)
    extend(-1, 3, Q)
    take(4, 0)
    begin(1, 1, A)
    take(4, 1)
    begin(-1, 1, B)
    moments_half(0, 1)
    extend(-1, 3, A)
    add_sibling(0)
    give(1, 1)
    give(-1, 1)
    give(0, 1)
    take(2, 1)
    extend(1, 3, B)
    extend(1, 4, Q)
    extend(-1, 4, Q)
    extend(1, 3, A)
    take(-2, 1)
    extend(-1, 3, B)
    extend(-1, 4, A)
    take(1, 1)
    extend(1, 4, B)
    m_part(0, 1, 0)[...] = finish(Q)
    give(0, 0)
    extend(1, 4, A)
    take(-1, 1)
    extend(-1, 4, B)
    take(0, 1)
    sums_ref[part:, :] = finish(B)
    last = finish(A)
    here = xbuf.at[0, :, span(0)]
    landed(20, here)
    sums_ref[0:part, 0 : 2 * width] = last + here[...]

    for copy in sent:
        copy.wait_send()

    def stat_sent(t, carry):
        stat_copy(0, t).wait_send()
        stat_copy(1, t).wait_send()
        return carry

    lax.fori_loop(1, n_comp, stat_sent, 0)


def solution(mesh):
    n_dp, n_comp = mesh.shape["dp"], mesh.shape["comp"]
    n_z = n_dp // 4

    def per_device(embeddings, comp_means, comp_variances, comp_mass):
        rows, width = embeddings.shape
        own = comp_means.shape[0]
        group = own * n_dp
        wide = 2 * width + 128
        tiles = rows // 128
        f32, bf16 = jnp.float32, jnp.bfloat16
        vmem, dma = pltpu.VMEM, pltpu.SemaphoreType.DMA
        inside = pl.BlockSpec(memory_space=pltpu.VMEM)
        mass = comp_mass.reshape(1, own)
        sums = pl.pallas_call(
            functools.partial(kernel, n_z, n_comp),
            out_shape=jax.ShapeDtypeStruct((own, wide), f32),
            in_specs=[pl.BlockSpec(memory_space=pl.ANY), inside, inside, inside],
            out_specs=inside,
            scratch_shapes=[
                vmem((rows, width), f32),
                vmem((group, wide), f32),
                vmem((24 * own, 2 * width), bf16),
                vmem((group, 128), f32),
                vmem((rows, 2 * width), bf16),
                vmem((rows, 2 * width), bf16),
                vmem((group, rows), f32),
                vmem((2, n_comp, tiles // 2, 128), f32),
                vmem((tiles, 128), f32),
                vmem((2 * group, rows), bf16),
                vmem((group, wide), f32),
                vmem((group // 2, wide), f32),
                vmem((22, own // 2, wide), f32),
                vmem((10, own // 2, wide), f32),
                dma, dma((40,)), dma((40,)), dma((2, n_comp)), dma((2, n_comp)), dma((40,)), dma((40,)),
            ],
            compiler_params=pltpu.CompilerParams(
                collective_id=0, has_side_effects=True, vmem_limit_bytes=56 * 1024 * 1024
            ),
        )(embeddings, comp_means, comp_variances, mass)
        new_means, new_variances, new_mass = pl.pallas_call(
            functools.partial(update, (group * n_comp) / (rows * n_dp)),
            out_shape=[
                jax.ShapeDtypeStruct((own, width), f32),
                jax.ShapeDtypeStruct((own, width), f32),
                jax.ShapeDtypeStruct((1, own), f32),
            ],
            in_specs=[inside] * 4,
            out_specs=[inside] * 3,
        )(sums, comp_means, comp_variances, mass)
        return new_means, new_variances, new_mass.reshape(own)

    placed = (P("dp", None), P(("comp", "dp"), None), P(("comp", "dp"), None), P(("comp", "dp")))
    return jax.shard_map(
        per_device,
        mesh=mesh,
        in_specs=placed,
        out_specs=(P(("comp", "dp"), None), P(("comp", "dp"), None), P(("comp", "dp"))),
        check_vma=False,
    )
```
